128 devices in a mesh: grp: 4 (over y), cur: 32 (over x, z, core).
Axes of the slice: x: 4, y: 4, z: 4, core: 2. Of those that a mesh axis runs over, the one named last changes fastest.
Arguments:
- fine_state: bfloat16 [786432, 256], P(('grp', 'cur')), may hold values from -8 to 8
- send_index: int32 [128, 2, 256], P(('grp', 'cur')), may hold values from 0 to 6143
- edge_src: int32 [128, 36864], P(('grp', 'cur')), may hold values from 0 to 6655, as said below
- edge_dst: int32 [128, 36864], P(('grp', 'cur')), may hold values from 0 to 6144, as said below
- cell_slot: int32 [786432], P(('grp', 'cur')), may hold values from 0 to 96, as said below
- slot_parent: int32 [128, 97], P(('grp', 'cur')), may hold values from 0 to 3071, as said below
- w_src: bfloat16 [256, 256], replicated, may hold values from -0.375 to 0.375
- w_dst: bfloat16 [256, 256], replicated, may hold values from -0.375 to 0.375
- msg_bias: float32 [256], replicated, may hold values from -4 to 4
- w_msg: bfloat16 [256, 256], replicated, may hold values from -0.375 to 0.375
- w_upd: bfloat16 [256, 256], replicated, may hold values from -0.375 to 0.375
- w_pool: bfloat16 [256, 1024], replicated, may hold values from -3 to 3
- norm_gain: float32 [1024], replicated, may hold values from 0.1 to 1.9
- w_query: bfloat16 [1024, 1024], replicated, may hold values from -1 to 1
- w_key: bfloat16 [1024, 256], replicated, may hold values from -1 to 1
- w_value: bfloat16 [1024, 256], replicated, may hold values from -0.1875 to 0.1875
- w_out: bfloat16 [1024, 1024], replicated, may hold values from -0.1875 to 0.1875
- head_scale: float32 [8], replicated, may hold values from 2 to 16
Outputs:
- fine_out: bfloat16 [786432, 256], P(('grp', 'cur'))
- coarse_out: bfloat16 [12288, 1024], P(('grp', 'cur'))
The draws below stay inside these ranges and needn't reach their ends.
Inputs may be any that keep to these rules, and one draw needn't show every extreme that they name: `edge_src`: slots from a device's live count on hold 0; live slots name any entry of the device's table. `edge_dst`: the value 6144 marks a padded slot. On each device the live slots come first and number between half of 36864 and all of it; some device has all slots live. `cell_slot`: cells of one device that share a slot are consecutive and have one parent; every slot 0 to 96 is used on every device. `slot_parent`: A parent numbered p within its group is owned by the device of that group with cur index p // 96, at row p % 96. Each of a group's parents has exactly 64 cells, all on one device or on two consecutive devices of the group. On each device at most 4 slots name parents of one owner, and some owner receives exactly 4 from every device of its group.
All inputs are finite; a program needn't handle non-finite values.
Results may differ from the reference program's by a relative error of at most 0.005.
Values may be sent and summed in bfloat16 or wider, within the bound.
No kernel may reach another device: no remote copies, remote signals or barrier semaphores. Data moves between devices by JAX's collectives and lax.ppermute only.
A program may use at most 128 MiB of HBM per device.

```python
import math
import jax
import jax.numpy as jnp
from jax import lax

F = 256
DC = 1024
HEADS = 8
KVH = 2
HD = 128
GR = 4
CHILD = 64
PAR_DEV = 96
HALO = 256
CELL_DEV = 6144
EDGE_DEV = 36864
CELLS = 786432
PAR_ALL = 12288
N_GRP = 4
N_CUR = 32


def live_slots(key):
    devices = N_GRP * N_CUR
    count = jax.random.randint(jax.random.fold_in(key, 11), (devices,), EDGE_DEV // 2, EDGE_DEV + 1)
    fullest = jax.random.randint(jax.random.fold_in(key, 12), (), 0, devices)
    count = jnp.where(jnp.arange(devices) == fullest, EDGE_DEV, count)
    return jnp.arange(EDGE_DEV)[None, :] < count[:, None]


def curve_layout(key):
    offset = jax.random.randint(jax.random.fold_in(key, 21), (N_GRP,), 1, CHILD)
    owner_keys = jax.random.split(jax.random.fold_in(key, 22), N_GRP)
    owners = jax.vmap(lambda k: jax.random.permutation(k, N_CUR))(owner_keys)
    row_keys = jax.random.split(jax.random.fold_in(key, 23), N_GRP)
    rows = jax.vmap(lambda k: jax.random.permutation(k, PAR_DEV))(row_keys)
    return (offset.astype(jnp.int32), owners.astype(jnp.int32), rows.astype(jnp.int32))


def regional_cells(key, noise, region_scale):
    regions = jax.random.normal(jax.random.fold_in(key, 41), (CELLS // CHILD, 1, F), jnp.float32) * region_scale
    spread = jnp.broadcast_to(regions, (CELLS // CHILD, CHILD, F)).reshape(CELLS, F)
    return jnp.clip(noise + spread, -8.0, 8.0)


def draw_fine_state(key, part):
    key = jax.random.fold_in(key, 7)
    noise = jax.random.normal(jax.random.fold_in(key, 42), (CELLS, F), jnp.float32)
    cells = regional_cells(key, noise, 1.2)
    return cells.astype(jnp.bfloat16)


def draw_edge_src(key, part):
    live = live_slots(key)
    key = jax.random.fold_in(key, 1)
    source = jax.random.randint(key, (N_GRP * N_CUR, EDGE_DEV), 0, CELL_DEV + 2 * HALO)
    return jnp.where(live, source, 0).astype(jnp.int32)


def draw_edge_dst(key, part):
    live = live_slots(key)
    key = jax.random.fold_in(key, 2)
    target = jax.random.randint(key, (N_GRP * N_CUR, EDGE_DEV), 0, CELL_DEV)
    return jnp.where(live, target, CELL_DEV).astype(jnp.int32)


def draw_cell_slot(key, part):
    offset, owners, rows = curve_layout(key)
    position = jnp.arange(CELL_DEV, dtype=jnp.int32)
    slot = (position[None, None, :] + offset[:, None, None]) // CHILD
    slot = jnp.broadcast_to(slot, (N_GRP, N_CUR, CELL_DEV))
    return slot.reshape(N_GRP * N_CUR * CELL_DEV).astype(jnp.int32)


def draw_slot_parent(key, part):
    offset, owners, rows = curve_layout(key)
    curve = jnp.arange(N_CUR, dtype=jnp.int32)[:, None] * PAR_DEV + jnp.arange(PAR_DEV + 1, dtype=jnp.int32)[None, :]
    curve = curve % (N_CUR * PAR_DEV)
    owner = jnp.take_along_axis(owners, jnp.broadcast_to((curve % N_CUR).reshape(1, -1), (N_GRP, curve.size)), axis=1)
    row = jnp.take_along_axis(rows, jnp.broadcast_to((curve // N_CUR).reshape(1, -1), (N_GRP, curve.size)), axis=1)
    parent = owner * PAR_DEV + row
    return parent.reshape(N_GRP * N_CUR, PAR_DEV + 1).astype(jnp.int32)


def query_base(key):
    base = jax.random.normal(jax.random.fold_in(key, 31), (DC, DC), jnp.float32) * DC ** (-0.5)
    return jnp.clip(base, -1.0, 1.0)


def draw_w_query(key, part):
    base = query_base(key)
    return base.astype(jnp.bfloat16)


def draw_w_key(key, part):
    key = jax.random.fold_in(key, 6)
    noise = jax.random.normal(key, (DC, KVH * HD), jnp.float32) * DC ** (-0.5)
    mixed = noise
    return jnp.clip(mixed, -1.0, 1.0).astype(jnp.bfloat16)


def set_ends(values, own_key, low, high):
    extent = values.shape
    index_at = [jax.random.randint(jax.random.fold_in(own_key, axis), (), 0, extent[axis]) for axis in range(len(extent))]
    values = values.at[tuple(index_at)].set(low)
    longest = extent.index(max(extent))
    index_at[longest] = (index_at[longest] + 1) % extent[longest]
    return values.at[tuple(index_at)].set(high)


def bell_draw(key, shape, deviation, most, kind=jnp.bfloat16):
    drawn = jax.random.normal(key, shape, jnp.float32) * deviation
    return jnp.minimum(jnp.maximum(drawn, -most), most).astype(kind)


def setup_inputs(seed: int = 0) -> dict:
    arg_keys = jax.random.split(jax.random.key(seed), 19)
    fine_state = draw_fine_state(jax.random.fold_in(arg_keys[18], 71), 0)
    send_index = set_ends(jax.random.randint(arg_keys[1], (N_GRP * N_CUR, 2, HALO), 0, CELL_DEV), jax.random.fold_in(arg_keys[1], 1), 0, CELL_DEV - 1).astype(jnp.int32)
    edge_src = draw_edge_src(jax.random.fold_in(arg_keys[18], 71), 0)
    edge_dst = draw_edge_dst(jax.random.fold_in(arg_keys[18], 71), 0)
    cell_slot = draw_cell_slot(jax.random.fold_in(arg_keys[18], 71), 0)
    slot_parent = draw_slot_parent(jax.random.fold_in(arg_keys[18], 71), 0)
    w_src = bell_draw(arg_keys[6], (F, F), F ** -0.5, 0.375)
    w_dst = bell_draw(arg_keys[7], (F, F), F ** -0.5, 0.375)
    msg_bias = bell_draw(arg_keys[8], (F,), 1.0, 4.0, jnp.float32)
    w_msg = bell_draw(arg_keys[9], (F, F), F ** -0.5, 0.375)
    w_upd = bell_draw(arg_keys[10], (F, F), F ** -0.5, 0.375)
    w_pool = bell_draw(arg_keys[11], (F, DC), (max(F // 64, 1)) ** -0.5, 3.0)
    norm_gain = jnp.clip(1.0 + 0.18 * jax.random.normal(arg_keys[12], (DC,), jnp.float32), 0.1, 1.9)
    w_query = draw_w_query(jax.random.fold_in(arg_keys[18], 71), 0)
    w_key = draw_w_key(jax.random.fold_in(arg_keys[18], 71), 0)
    w_value = bell_draw(arg_keys[15], (DC, KVH * HD), DC ** -0.5, 0.1875)
    w_out = bell_draw(arg_keys[16], (DC, DC), DC ** -0.5, 0.1875)
    head_scale = jnp.clip(jnp.exp(jax.random.uniform(arg_keys[17], (HEADS,), jnp.float32, math.log(2.0), math.log(16.0))), 2.0, 16.0)
    return {"fine_state": fine_state, "send_index": send_index, "edge_src": edge_src, "edge_dst": edge_dst, "cell_slot": cell_slot, "slot_parent": slot_parent, "w_src": w_src, "w_dst": w_dst, "msg_bias": msg_bias, "w_msg": w_msg, "w_upd": w_upd, "w_pool": w_pool, "norm_gain": norm_gain, "w_query": w_query, "w_key": w_key, "w_value": w_value, "w_out": w_out, "head_scale": head_scale}


def reference(fine_state, send_index, edge_src, edge_dst, cell_slot, slot_parent, w_src, w_dst, msg_bias, w_msg, w_upd, w_pool, norm_gain, w_query, w_key, w_value, w_out, head_scale):
    devices = N_GRP * N_CUR
    cells = fine_state.reshape(devices, CELL_DEV, F)
    sent = jax.vmap(lambda rows, picks: rows[picks])(cells, send_index)
    from_prev = jnp.roll(sent[:, 0], 1, axis=0)
    from_next = jnp.roll(sent[:, 1], -1, axis=0)

    def fine_layer(inputs):
        own, before, after, source, target = inputs
        table = jnp.concatenate([own, before, after], axis=0)
        src_proj = jnp.dot(table, w_src, preferred_element_type=jnp.float32).astype(jnp.bfloat16)
        dst_proj = jnp.dot(own, w_dst, preferred_element_type=jnp.float32).astype(jnp.bfloat16)
        clipped = jnp.minimum(target, CELL_DEV - 1)
        pre = src_proj[source].astype(jnp.float32) + dst_proj[clipped].astype(jnp.float32) + msg_bias
        hidden = jax.nn.silu(pre).astype(jnp.bfloat16)
        message = jnp.dot(hidden, w_msg, preferred_element_type=jnp.float32)
        total = jax.ops.segment_sum(message, target, num_segments=CELL_DEV + 1)[:CELL_DEV]
        count = jax.ops.segment_sum(jnp.ones(target.shape, jnp.float32), target, num_segments=CELL_DEV + 1)[:CELL_DEV]
        agg = (total / jnp.maximum(count, 1.0)[:, None]).astype(jnp.bfloat16)
        update = jnp.dot(agg, w_upd, preferred_element_type=jnp.float32)
        return (own.astype(jnp.float32) + update).astype(jnp.bfloat16)
    fine_out = lax.map(fine_layer, (cells, from_prev, from_next, edge_src, edge_dst)).reshape(CELLS, F)
    group = jnp.arange(devices, dtype=jnp.int32) // N_CUR
    parent_dev = slot_parent + (group * (N_CUR * PAR_DEV))[:, None]
    slots = cell_slot.reshape(devices, CELL_DEV)
    parent_cell = jnp.take_along_axis(parent_dev, slots, axis=1).reshape(CELLS).astype(jnp.int32)
    parent_sum = jax.ops.segment_sum(fine_out.astype(jnp.float32), parent_cell, num_segments=PAR_ALL)
    parent_mean = (parent_sum / float(CHILD)).astype(jnp.bfloat16)
    coarse = jnp.dot(parent_mean, w_pool, preferred_element_type=jnp.float32)
    inverse = lax.rsqrt(lax.optimization_barrier(jnp.mean(coarse * coarse, axis=1, keepdims=True)) + 1e-06)
    normed = (coarse * inverse * norm_gain).astype(jnp.bfloat16)
    query = jnp.dot(normed, w_query, preferred_element_type=jnp.float32).astype(jnp.bfloat16)
    keys = jnp.dot(normed, w_key, preferred_element_type=jnp.float32).astype(jnp.bfloat16)
    values = jnp.dot(normed, w_value, preferred_element_type=jnp.float32).astype(jnp.bfloat16)
    key_all = keys.astype(jnp.float32).reshape(PAR_ALL, KVH, HD)
    value_all = values.astype(jnp.float32).reshape(PAR_ALL, KVH, HD)
    factor = (head_scale * (1.0 / math.sqrt(HD))).reshape(KVH, GR)

    def attend(block):
        qblock = block.astype(jnp.float32).reshape(PAR_DEV, KVH, GR, HD)
        score = jnp.einsum('qgrd,kgd->grqk', qblock, key_all) * factor[:, :, None, None]
        top = lax.optimization_barrier(jnp.max(score, axis=-1, keepdims=True))
        weight = jnp.exp(score - top)
        norm = lax.optimization_barrier(jnp.sum(weight, axis=-1))
        rounded = weight.astype(jnp.bfloat16).astype(jnp.float32)
        numer = jnp.einsum('grqk,kgd->qgrd', rounded, value_all)
        attn = numer / jnp.transpose(norm, (2, 0, 1))[..., None]
        return attn.reshape(PAR_DEV, DC).astype(jnp.bfloat16)
    attn = lax.map(attend, query.reshape(PAR_ALL // PAR_DEV, PAR_DEV, DC)).reshape(PAR_ALL, DC)
    coarse_out = (coarse + jnp.dot(attn, w_out, preferred_element_type=jnp.float32)).astype(jnp.bfloat16)
    return (fine_out, coarse_out)
```

```python
import math
import jax, jax.numpy as jnp
from jax import lax
from jax.experimental import pallas as pl
from jax.experimental.pallas import tpu as pltpu
from jax.sharding import PartitionSpec as P

TILE = 256
BLOCK_SHIFT = 22
LOCAL_SHIFT = 13
SLOT_ROWS = 104
bf16, f32, i32 = jnp.bfloat16, jnp.float32, jnp.int32


def sort_edges(source, target, blocks):
    edges = source.shape[0]
    block = target >> 8
    last = (blocks - 1) << BLOCK_SHIFT | 511 << LOCAL_SHIFT
    key = jnp.where(target < blocks * TILE,
                    (block << BLOCK_SHIFT) | ((target & 255) << LOCAL_SHIFT) | source, last)
    block_ids = jnp.arange(blocks, dtype=i32)
    count = jnp.sum((block[None, :] == block_ids[:, None]).astype(i32), axis=1)
    spare = (-count) & (TILE - 1)
    lane = jnp.arange(TILE, dtype=i32)
    filler = jnp.where(lane[None, :] < spare[:, None], (block_ids[:, None] << BLOCK_SHIFT) | (256 << LOCAL_SHIFT), last)
    keys = jnp.sort(jnp.concatenate([key, filler.reshape(-1)]))
    tiles = jnp.sum((count + spare) // TILE)
    return keys, tiles


def fine_kernel(rows_ref, meta_ref, local_ref, slot_ref, tag_ref, own_ref, before_ref, after_ref, w_src_ref, w_dst_ref,
                bias_ref, w_msg_ref, w_upd_ref, out_ref, part_ref, table, dst, total, count, got_a, got_b):
    blocks = own_ref.shape[0] // TILE
    tiles_most = local_ref.shape[0]

    def put_table(place, rows):
        proj = jnp.dot(rows, w_src_ref[...], preferred_element_type=f32).astype(bf16).astype(f32) + bias_ref[...]
        table[pl.ds(2 * place, TILE, stride=2), :] = proj[:, :128]
        table[pl.ds(2 * place + 1, TILE, stride=2), :] = proj[:, 128:]

    def project(b, carry):
        at = pl.multiple_of(b * TILE, TILE)
        own = own_ref[pl.ds(at, TILE), :]
        put_table(at, own)
        dst[pl.ds(at, TILE), :] = jnp.dot(own, w_dst_ref[...], preferred_element_type=f32).astype(bf16)
        total[pl.ds(at, TILE), :] = jnp.zeros((TILE, 256), f32)
        count[b] = jnp.zeros((8, TILE), f32)
        return carry

    lax.fori_loop(0, blocks, project, 0)
    put_table(blocks * TILE, before_ref[...])
    put_table(blocks * TILE + TILE, after_ref[...])

    def fetch(tile, got):
        base = jnp.minimum(tile, tiles_most - 1) * TILE
        for i in range(TILE):
            got[2 * i:2 * i + 2, :] = table[pl.ds(rows_ref[base + i], 2), :]

    rows_iota = lax.broadcasted_iota(i32, (TILE, TILE), 0)

    def dense(tile, got):
        b = meta_ref[tile]
        at = pl.multiple_of(b * TILE, TILE)
        hot = (rows_iota == local_ref[tile]).astype(f32).astype(bf16)
        own = lax.dot_general(hot, dst[pl.ds(at, TILE), :], (((0,), (0,)), ((), ())), preferred_element_type=f32)
        pre = own + jnp.concatenate([got[pl.ds(0, TILE, stride=2), :], got[pl.ds(1, TILE, stride=2), :]], axis=1)
        half = 0.5 * pre
        hidden = (half + half * jnp.tanh(half)).astype(bf16)
        total[pl.ds(at, TILE), :] += jnp.dot(hot, hidden, preferred_element_type=f32)
        count[b] += lax.dot_general(jnp.ones((8, TILE), bf16), hot, (((1,), (1,)), ((), ())), preferred_element_type=f32)

    fetch(0, got_a)

    def step(j, carry):
        fetch(2 * j + 1, got_b)
        dense(2 * j, got_a)
        fetch(2 * j + 2, got_a)
        dense(2 * j + 1, got_b)
        return carry

    lax.fori_loop(0, meta_ref[tiles_most], step, 0)

    slots = lax.broadcasted_iota(i32, (SLOT_ROWS, TILE), 0)

    def finish(b, parts):
        at = pl.multiple_of(b * TILE, TILE)
        scale = 1.0 / jnp.maximum(count[b], 1.0)
        scale = jnp.transpose(jnp.concatenate([scale] * 16, axis=0))
        mean = total[pl.ds(at, TILE), :] * jnp.concatenate([scale, scale], axis=1)
        high = mean.astype(bf16)
        low = (mean - high.astype(f32)).astype(bf16)
        w_msg = w_msg_ref[...]
        agg = (jnp.dot(high, w_msg, preferred_element_type=f32) + jnp.dot(low, w_msg, preferred_element_type=f32)).astype(bf16)
        update = jnp.dot(agg, w_upd_ref[...], preferred_element_type=f32)
        new = (own_ref[pl.ds(at, TILE), :].astype(f32) + update).astype(bf16)
        out_ref[pl.ds(at, TILE), :] = new
        hot = (slots == slot_ref[b]).astype(f32).astype(bf16)
        return parts + jnp.dot(hot, new, preferred_element_type=f32)

    parts = lax.fori_loop(0, blocks, finish, tag_ref[...].astype(f32))
    part_ref[...] = parts.astype(bf16)


def fine_pass(own, before, after, source, target, cell_slot, tags, w_src, w_dst, bias, w_msg, w_upd):
    cells = own.shape[0]
    blocks = cells // TILE
    keys, tiles = sort_edges(source, target, blocks)
    tiles_most = keys.shape[0] // TILE
    rows = (keys & ((1 << LOCAL_SHIFT) - 1)) * 2
    local = ((keys >> LOCAL_SHIFT) & 511).reshape(tiles_most, 1, TILE)
    meta = jnp.concatenate([keys[::TILE] >> BLOCK_SHIFT, ((tiles + 1) // 2)[None]])
    smem = pl.BlockSpec(memory_space=pltpu.SMEM)
    vmem = pl.BlockSpec(memory_space=pltpu.VMEM)
    return pl.pallas_call(
        fine_kernel,
        out_shape=(jax.ShapeDtypeStruct(own.shape, bf16), jax.ShapeDtypeStruct((SLOT_ROWS, 256), bf16)),
        in_specs=[smem, smem] + [vmem] * 11,
        out_specs=(vmem, vmem),
        scratch_shapes=[
            pltpu.VMEM((2 * (cells + 2 * TILE), 128), f32),
            pltpu.VMEM((cells, 256), bf16),
            pltpu.VMEM((cells, 256), f32),
            pltpu.VMEM((blocks, 8, TILE), f32),
            pltpu.VMEM((2 * TILE, 128), f32),
            pltpu.VMEM((2 * TILE, 128), f32),
        ],
        compiler_params=pltpu.CompilerParams(vmem_limit_bytes=56 << 20),
        name="fine_cells",
    )(rows, meta, local, cell_slot.reshape(blocks, 1, TILE), tags, own, before, after, w_src, w_dst, bias.reshape(1, -1), w_msg, w_upd)


def moved(value, axis, pairs):
    return lax.ppermute(value, axis, pairs)


def ring_gather(value, move):
    return jnp.concatenate([value] + [move(value, by) for by in (1, 3, 2)], axis=0)


def gather_group(part):
    devices = lax.axis_size("cur")

    def along_z(value, by):
        return lax.ppermute(value, "cur", [(i, i // 8 * 8 + (i + 2 * by) % 8) for i in range(devices)])

    def along_x(value, by):
        return lax.ppermute(value, "cur", [(i, (i + 8 * by) % devices) for i in range(devices)])

    rows = ring_gather(part[None], along_z)
    rows = ring_gather(rows, along_x)
    return jnp.concatenate([rows, lax.ppermute(rows, "cur", [(i, i ^ 1) for i in range(devices)])], axis=0)


def normed_parents(first, label_ref, rows_ref, w_pool_ref, gain_ref, parents):
    ids = lax.broadcasted_iota(i32, (parents, rows_ref.shape[0]), 0) + first
    hot = (ids == label_ref[...]).astype(f32).astype(bf16)
    mean = (jnp.dot(hot, rows_ref[...], preferred_element_type=f32) * (1.0 / 64.0)).astype(bf16)
    coarse = jnp.dot(mean, w_pool_ref[...], preferred_element_type=f32)
    inverse = lax.rsqrt(jnp.mean(coarse * coarse, axis=1, keepdims=True) + 1e-06)
    return coarse, (coarse * inverse * gain_ref[...]).astype(bf16)


def query_kernel(first_ref, label_ref, rows_ref, w_pool_ref, gain_ref, w_query_ref, coarse_ref, query_ref):
    coarse, normed = normed_parents(first_ref[0], label_ref, rows_ref, w_pool_ref, gain_ref, query_ref.shape[0])
    coarse_ref[...] = coarse
    query_ref[...] = jnp.dot(normed, w_query_ref[...], preferred_element_type=f32).astype(bf16)


def key_kernel(label_ref, rows_ref, w_pool_ref, gain_ref, w_key_ref, w_value_ref, key_ref, value_ref):
    parents = value_ref.shape[1]
    coarse, normed = normed_parents(pl.program_id(0) * parents, label_ref, rows_ref, w_pool_ref, gain_ref, parents)
    keys = jnp.dot(normed, w_key_ref[...], preferred_element_type=f32)
    values = jnp.dot(normed, w_value_ref[...], preferred_element_type=f32).astype(bf16)
    ones = jnp.ones((parents, 128), bf16)
    for g in range(2):
        turned = jnp.transpose(keys[:, g * 128:(g + 1) * 128]).astype(bf16)
        key_ref[g] = jnp.concatenate([turned, turned], axis=0)
        value_ref[g] = jnp.concatenate([values[:, g * 128:(g + 1) * 128], ones], axis=1)


def attend_kernel(factor_ref, query_ref, key_ref, value_ref, out_ref):
    rows = query_ref.shape[0]
    stats = []
    for g in range(2):
        scaled = jnp.concatenate(
            [query_ref[:, h * 128:(h + 1) * 128].astype(f32) * factor_ref[h] for h in range(4 * g, 4 * g + 4)], axis=0
        )
        high = scaled.astype(bf16)
        low = (scaled - high.astype(f32)).astype(bf16)
        score = jnp.dot(jnp.concatenate([high, low], axis=1), key_ref[g], preferred_element_type=f32)
        top = jnp.max(score, axis=1, keepdims=True)
        weight = jnp.exp2(score - top).astype(bf16)
        both = jnp.dot(weight, value_ref[g], preferred_element_type=f32)
        norm = both[:, 128:]
        attn = (both[:, :128] / norm).astype(bf16)
        level = top + jnp.log2(norm)
        for r in range(4):
            h = 4 * g + r
            out_ref[:, h * 128:(h + 1) * 128] = attn[r * rows:(r + 1) * rows]
            stats.append(level[r * rows:(r + 1) * rows])
    lanes = lax.broadcasted_iota(i32, (rows, 128), 1)
    level = jnp.zeros((rows, 128), f32)
    for h in range(8):
        level = jnp.where(lanes == h, stats[h], level)
    high = level.astype(bf16)
    rest = level - high.astype(f32)
    middle = rest.astype(bf16)
    low = (rest - middle.astype(f32)).astype(bf16)
    out_ref[:, 1024:1152] = high
    out_ref[:, 1152:1280] = middle
    out_ref[:, 1280:1408] = low


def merge_kernel(a_ref, b_ref, c_ref, d_ref, coarse_ref, w_out_ref, out_ref):
    refs = (a_ref, b_ref, c_ref, d_ref)
    levels = [r[:, 1024:1152].astype(f32) + (r[:, 1152:1280].astype(f32) + r[:, 1280:1408].astype(f32)) for r in refs]
    top = jnp.maximum(jnp.maximum(levels[0], levels[1]), jnp.maximum(levels[2], levels[3]))
    shares = [jnp.exp2(level - top) for level in levels]
    whole = shares[0] + shares[1] + shares[2] + shares[3]
    shares = [share / whole for share in shares]
    pieces = []
    for h in range(8):
        at = slice(h * 128, (h + 1) * 128)
        pieces.append(sum(r[:, at].astype(f32) * s[:, h:h + 1] for r, s in zip(refs, shares)))
    attn = jnp.concatenate(pieces, axis=1).astype(bf16)
    out_ref[...] = (coarse_ref[...] + jnp.dot(attn, w_out_ref[...], preferred_element_type=f32)).astype(bf16)


def body(fine_state, send_index, edge_src, edge_dst, cell_slot, slot_parent, w_src, w_dst, msg_bias, w_msg, w_upd,
         w_pool, norm_gain, w_query, w_key, w_value, w_out, head_scale):
    groups, devices = lax.axis_size("grp"), lax.axis_size("cur")
    smem = pl.BlockSpec(memory_space=pltpu.SMEM)
    vmem = pl.BlockSpec(memory_space=pltpu.VMEM)
    every = groups * devices
    both = ("grp", "cur")
    before = lax.ppermute(fine_state[send_index[0, 0]], both, [(i, (i + 1) % every) for i in range(every)])
    after = lax.ppermute(fine_state[send_index[0, 1]], both, [(i, (i - 1) % every) for i in range(every)])
    slots = slot_parent.shape[1]
    par_dev = slots - 1
    parents = jnp.full((256,), -64, i32).at[:slots].set(slot_parent[0])
    tags = jnp.zeros((SLOT_ROWS, 256), i32).at[slots].set(parents >> 6).at[slots + 1].set(parents & 63).astype(bf16)
    fine_out, part = fine_pass(fine_state, before, after, edge_src[0], edge_dst[0], cell_slot, tags,
                               w_src, w_dst, msg_bias, w_msg, w_upd)
    blocks = gather_group(part)
    labels = (blocks[:, slots, :SLOT_ROWS].astype(i32) * 64 + blocks[:, slots + 1, :SLOT_ROWS].astype(i32)).reshape(1, -1)
    rows = blocks.reshape(-1, 256)
    gain = norm_gain.reshape(1, -1)
    width = w_query.shape[1]
    params = pltpu.CompilerParams(vmem_limit_bytes=56 << 20)
    coarse, query = pl.pallas_call(
        query_kernel,
        out_shape=(jax.ShapeDtypeStruct((par_dev, width), f32), jax.ShapeDtypeStruct((par_dev, width), bf16)),
        in_specs=[smem] + [vmem] * 5,
        out_specs=(vmem, vmem),
        compiler_params=params,
        name="own_query",
    )((lax.axis_index("cur") * par_dev)[None], labels, rows, w_pool, gain, w_query)
    asked = {by: lax.ppermute(query, "grp", [(i, (i + by) % groups) for i in range(groups)]) for by in (2, 1, 3)}
    asked[0] = query
    known = par_dev * devices
    step = 512
    whole = lambda *shape: pl.BlockSpec(shape, lambda i: (0,) * len(shape))
    keys, values = pl.pallas_call(
        key_kernel,
        out_shape=(jax.ShapeDtypeStruct((2, 256, known), bf16), jax.ShapeDtypeStruct((2, known, 256), bf16)),
        grid=(known // step,),
        in_specs=[whole(*labels.shape), whole(*rows.shape), whole(*w_pool.shape), whole(*gain.shape),
                  whole(*w_key.shape), whole(*w_value.shape)],
        out_specs=(pl.BlockSpec((2, 256, step), lambda i: (0, 0, i)), pl.BlockSpec((2, step, 256), lambda i: (0, i, 0))),
        compiler_params=params,
        name="group_keys",
    )(labels, rows, w_pool, gain, w_key, w_value)
    factor = head_scale * (math.log2(math.e) / math.sqrt(128.0))
    found = []
    for by in (2, 1, 3, 0):
        piece = pl.pallas_call(
            attend_kernel,
            out_shape=jax.ShapeDtypeStruct((par_dev, width + 384), bf16),
            in_specs=[smem] + [vmem] * 3,
            out_specs=vmem,
            compiler_params=params,
            name="attend",
        )(factor, asked[by], keys, values)
        if by:
            piece = lax.ppermute(piece, "grp", [(i, (i - by) % groups) for i in range(groups)])
        found.append(piece)
    coarse_out = pl.pallas_call(
        merge_kernel,
        out_shape=jax.ShapeDtypeStruct((par_dev, width), bf16),
        in_specs=[vmem] * 6,
        out_specs=vmem,
        compiler_params=params,
        name="merge",
    )(*found, coarse, w_out)
    return fine_out, coarse_out


def solution(mesh):
    line = P(("grp", "cur"), None)
    in_specs = (line, P(("grp", "cur"), None, None), line, line, P(("grp", "cur")), line) + (P(),) * 12
    return jax.shard_map(body, mesh=mesh, in_specs=in_specs, out_specs=(line, line), check_vma=False)
```

```python
import functools
import math
import jax, jax.numpy as jnp
from jax import lax
from jax.experimental import pallas as pl
from jax.experimental.pallas import tpu as pltpu
from jax.sharding import PartitionSpec as P

TILE = 256
WINDOW = 128
TOGETHER = 4
TARGET_SHIFT = 13
NO_TARGET = 6144
SLOT_ROWS = 104
bf16, f32, i32 = jnp.bfloat16, jnp.float32, jnp.int32


def sort_kernel(source_ref, target_ref, rows_ref, targets_ref, key):
    given = source_ref.shape[0]
    fill = jnp.full((8, 128), NO_TARGET << TARGET_SHIFT, i32)
    held = [(target_ref[v] << TARGET_SHIFT) | source_ref[v] if v < given else fill for v in range(64)]
    for phase in range(1, 6):
        for bit in range(phase - 1, -1, -1):
            for v in range(64):
                if not v >> bit & 1:
                    w = v | 1 << bit
                    small, large = jnp.minimum(held[v], held[w]), jnp.maximum(held[v], held[w])
                    held[v], held[w] = (large, small) if v >> phase & 1 else (small, large)
    for v in range(64):
        key[v >> 3, v & 7] = held[v]
    row = lax.broadcasted_iota(i32, (8, 128), 0)
    lane = lax.broadcasted_iota(i32, (8, 128), 1)

    def bit_of(bit):
        if bit == 16:
            return jnp.zeros((8, 128), i32)
        return (row >> (bit - 6) & 1) if bit < 9 else (lane >> (bit - 9) & 1)

    for phase in range(6, 17):
        flip = bit_of(phase) if phase == 6 else bit_of(phase) ^ bit_of(phase - 1)

        def across(g, carry):
            held = key[pl.ds(2 * g, 2)].reshape(16, 8, 128) ^ (-flip)[None]
            for bit in range(phase - 1, 5, -1):
                axis, by, size = (1, 1 << (bit - 6), 8) if bit < 9 else (2, 1 << (bit - 9), 128)
                upper = (bit_of(bit) == 1)[None]
                if 2 * by == size:
                    other = pltpu.roll(held, by, axis)
                else:
                    other = jnp.where(upper, pltpu.roll(held, by, axis), pltpu.roll(held, size - by, axis))
                held = jnp.where(upper, jnp.maximum(held, other), jnp.minimum(held, other))
            key[pl.ds(2 * g, 2)] = held.reshape(2, 8, 8, 128)
            return carry

        lax.fori_loop(0, 4, across, 0, unroll=4)

        def merge(held):
            for bit in (2, 1, 0):
                pairs = held.reshape(4 >> bit, 2, 1 << bit, 8, 128)
                held = jnp.stack(
                    [jnp.minimum(pairs[:, 0], pairs[:, 1]), jnp.maximum(pairs[:, 0], pairs[:, 1])], axis=1
                ).reshape(8, 8, 128)
            return held

        def high(g, carry):
            key[:, g] = merge(key[:, g])
            return carry

        def low(g, carry):
            key[g] = merge(key[g])
            return carry

        lax.fori_loop(0, 8, high, 0, unroll=8)
        lax.fori_loop(0, 8, low, 0, unroll=8)

    flat = key.reshape(512, 128)
    half = rows_ref.shape[1] // 2
    for part in range(4):
        piece = jnp.concatenate([flat[pl.ds(s, 64, stride=8), :] for s in (2 * part, 2 * part + 1)], axis=0)
        piece = jnp.transpose(piece)[:half]
        at = (part % 2, pl.ds(part // 2, half, stride=2), slice(None))
        rows_ref[at] = (piece & ((1 << TARGET_SHIFT) - 1)) * 2
        targets_ref[at] = piece >> TARGET_SHIFT


def sorted_edges(source, target):
    edges = source.shape[0]
    shape = jax.ShapeDtypeStruct((2, edges // TILE, 128), i32)
    return pl.pallas_call(
        sort_kernel,
        out_shape=(shape, shape),
        scratch_shapes=[pltpu.VMEM((8, 8, 8, 128), i32)],
        compiler_params=pltpu.CompilerParams(vmem_limit_bytes=24 << 20),
        name="sort_edges",
    )(source.reshape(-1, 8, 128), target.reshape(-1, 8, 128))


def fine_kernel(rows_ref, meta_ref, local_ref, slot_ref, tag_ref, own_ref, before_ref, after_ref, w_src_ref, w_dst_ref,
                bias_ref, w_msg_ref, w_upd_ref, out_ref, part_ref, table, dst, total, count, got_a, got_b):
    blocks = own_ref.shape[0] // TILE
    tiles_most = local_ref.shape[1]

    def put_table(place, rows):
        proj = jnp.dot(rows, w_src_ref[...], preferred_element_type=f32).astype(bf16).astype(f32) + bias_ref[...]
        table[pl.ds(2 * place, TILE, stride=2), :] = proj[:, :128]
        table[pl.ds(2 * place + 1, TILE, stride=2), :] = proj[:, 128:]

    def project(b, carry):
        at = pl.multiple_of(b * TILE, TILE)
        own = own_ref[pl.ds(at, TILE), :]
        put_table(at, own)
        dst[pl.ds(at, TILE), :] = jnp.dot(own, w_dst_ref[...], preferred_element_type=f32).astype(bf16)
        total[pl.ds(at, TILE), :] = jnp.zeros((TILE, 256), f32)
        count[pl.ds(at, TILE), :] = jnp.zeros((TILE, 128), f32)
        return carry

    lax.fori_loop(0, blocks, project, 0, unroll=4)
    put_table(blocks * TILE, before_ref[...])
    put_table(blocks * TILE + TILE, after_ref[...])

    place = lax.broadcasted_iota(i32, (WINDOW, TILE), 0).astype(f32).astype(bf16)
    one, zero = jnp.ones((WINDOW, TILE), bf16), jnp.zeros((WINDOW, TILE), bf16)
    ones = jnp.ones((TILE, 128), bf16)

    def fetch(base, first, last, got):
        for i in range(first, last):
            place = i % TILE // 128 * (tiles_most * 128) + i // TILE * 128 + i % 128
            got[2 * i:2 * i + 2, :] = table[pl.ds(rows_ref[base + place], 2), :]

    def tile_steps(tile, n, got, start):
        state = {}

        def first():
            state["at"] = at = pl.multiple_of(start, 16)
            local = jnp.concatenate([local_ref[k, pl.ds(tile, 1), :] for k in range(2)], axis=1)
            local = jnp.minimum(local - at, WINDOW).astype(f32).astype(bf16)
            state["hot"] = jnp.where(place == local, one, zero)
            state["own"] = lax.dot_general(
                state["hot"], dst[pl.ds(at, WINDOW), :], (((0,), (0,)), ((), ())), preferred_element_type=f32
            )

        def second():
            sent = [got[pl.ds(2 * TILE * n + k, TILE, stride=2), :] for k in range(2)]
            half = 0.5 * (state["own"] + jnp.concatenate(sent, axis=1))
            state["hidden"] = (half + half * jnp.tanh(half)).astype(bf16)

        def third():
            at = pl.ds(state["at"], WINDOW)
            total[at, :] += jnp.dot(state["hot"], state["hidden"], preferred_element_type=f32)
            count[at, :] += jnp.dot(state["hot"], ones, preferred_element_type=f32)

        return first, second, third

    def advance(tile, got, ahead, got_ahead):
        base = jnp.minimum(ahead, tiles_most - TOGETHER) * 128
        tiles = [tile_steps(tile + n, n, got, meta_ref[tile + n]) for n in range(TOGETHER)]
        steps = [run for steps in zip(*tiles) for run in steps]
        rows = TOGETHER * TILE
        for i, run in enumerate(steps):
            fetch(base, rows * i // len(steps), rows * (i + 1) // len(steps), got_ahead)
            run()

    def step(j, carry):
        tile = 2 * TOGETHER * j
        advance(tile, got_a, tile + TOGETHER, got_b)
        advance(tile + TOGETHER, got_b, tile + 2 * TOGETHER, got_a)
        return carry

    fetch(0, 0, TOGETHER * TILE, got_a)
    lax.fori_loop(0, meta_ref[2 * tiles_most], step, 0)

    def rest(tile, carry):
        def window(w, carry):
            fetch(tile * 128, 0, TILE, got_a)
            for run in tile_steps(tile, 0, got_a, jnp.minimum(meta_ref[tile] + w * WINDOW, blocks * TILE - WINDOW)):
                run()
            return carry

        return lax.fori_loop(1, meta_ref[tiles_most + tile], window, carry)

    lax.fori_loop(0, tiles_most, rest, 0)

    slots = lax.broadcasted_iota(i32, (SLOT_ROWS, TILE), 0)

    def finish(b, parts):
        at = pl.ds(pl.multiple_of(b * TILE, TILE), TILE)
        scale = 1.0 / jnp.maximum(count[at, :], 1.0)
        mean = total[at, :] * jnp.concatenate([scale, scale], axis=1)
        high = mean.astype(bf16)
        low = (mean - high.astype(f32)).astype(bf16)
        w_msg = w_msg_ref[...]
        agg = jnp.dot(high, w_msg, preferred_element_type=f32) + jnp.dot(low, w_msg, preferred_element_type=f32)
        update = jnp.dot(agg.astype(bf16), w_upd_ref[...], preferred_element_type=f32)
        new = (own_ref[at, :].astype(f32) + update).astype(bf16)
        out_ref[at, :] = new
        hot = (slots == slot_ref[b]).astype(f32).astype(bf16)
        return parts + jnp.dot(hot, new, preferred_element_type=f32)

    parts = lax.fori_loop(0, blocks, finish, tag_ref[...].astype(f32), unroll=4)
    part_ref[...] = parts.astype(bf16)


def fine_pass(own, before, after, source, target, cell_slot, tags, w_src, w_dst, bias, w_msg, w_upd):
    cells = own.shape[0]
    blocks = cells // TILE
    tiles = source.shape[0] // TILE
    rows, targets = sorted_edges(source, target)
    start = jnp.minimum(targets[0, :, 0] & -16, cells - WINDOW)
    last = jnp.max(jnp.where(targets < cells, targets, -1), axis=(0, 2))
    windows = jnp.maximum(last + WINDOW - start, 0) // WINDOW
    pairs = (jnp.sum((last >= 0).astype(i32)) + (2 * TOGETHER - 1)) // (2 * TOGETHER)
    meta = jnp.concatenate([start, windows, pairs[None]])
    smem = pl.BlockSpec(memory_space=pltpu.SMEM)
    vmem = pl.BlockSpec(memory_space=pltpu.VMEM)
    return pl.pallas_call(
        fine_kernel,
        out_shape=(jax.ShapeDtypeStruct(own.shape, bf16), jax.ShapeDtypeStruct((SLOT_ROWS, 256), bf16)),
        in_specs=[smem, smem] + [vmem] * 11,
        out_specs=(vmem, vmem),
        scratch_shapes=[
            pltpu.VMEM((2 * (cells + 2 * TILE), 128), f32),
            pltpu.VMEM((cells, 256), bf16),
            pltpu.VMEM((cells, 256), f32),
            pltpu.VMEM((cells, 128), f32),
            pltpu.VMEM((2 * TOGETHER * TILE, 128), f32),
            pltpu.VMEM((2 * TOGETHER * TILE, 128), f32),
        ],
        compiler_params=pltpu.CompilerParams(vmem_limit_bytes=58 << 20),
        name="fine_cells",
    )(rows.reshape(-1), meta, targets, cell_slot.reshape(blocks, 1, TILE), tags, own, before, after, w_src, w_dst,
      bias.reshape(1, -1), w_msg, w_upd)


def moved(value, axis, pairs):
    return lax.ppermute(value, axis, pairs)


def ring_gather(value, move):
    return jnp.concatenate([value] + [move(value, by) for by in (1, 3, 2)], axis=0)


def gather_group(part):
    devices = lax.axis_size("cur")

    def along_z(value, by):
        return lax.ppermute(value, "cur", [(i, i // 8 * 8 + (i + 2 * by) % 8) for i in range(devices)])

    def along_x(value, by):
        return lax.ppermute(value, "cur", [(i, (i + 8 * by) % devices) for i in range(devices)])

    rows = ring_gather(part[None], along_z)
    rows = ring_gather(rows, along_x)
    return jnp.concatenate([rows, lax.ppermute(rows, "cur", [(i, i ^ 1) for i in range(devices)])], axis=0)


def normed_parents(first, label_ref, rows_ref, w_pool_ref, gain_ref, parents):
    shape = (parents, rows_ref.shape[0])
    ids = lax.broadcasted_iota(i32, shape, 0).astype(f32).astype(bf16)
    label = jnp.clip(label_ref[...] - first, -1, 256).astype(f32).astype(bf16)
    hot = jnp.where(ids == label, jnp.ones(shape, bf16), jnp.zeros(shape, bf16))
    mean = (jnp.dot(hot, rows_ref[...], preferred_element_type=f32) * (1.0 / 64.0)).astype(bf16)
    coarse = jnp.dot(mean, w_pool_ref[...], preferred_element_type=f32)
    inverse = lax.rsqrt(jnp.mean(coarse * coarse, axis=1, keepdims=True) + 1e-06)
    return coarse, (coarse * inverse * gain_ref[...]).astype(bf16)


def query_kernel(first_ref, label_ref, rows_ref, w_pool_ref, gain_ref, w_query_ref, coarse_ref, query_ref):
    coarse, normed = normed_parents(first_ref[0], label_ref, rows_ref, w_pool_ref, gain_ref, query_ref.shape[0])
    coarse_ref[...] = coarse
    query_ref[...] = jnp.dot(normed, w_query_ref[...], preferred_element_type=f32).astype(bf16)


def key_kernel(first_ref, label_ref, rows_ref, w_pool_ref, gain_ref, w_key_ref, w_value_ref, key_ref, value_ref):
    most = 256
    for part in range(value_ref.shape[0] // most):
        at = slice(part * most, (part + 1) * most)
        first = first_ref[0] + pl.program_id(0) * value_ref.shape[0] + part * most
        coarse, normed = normed_parents(first, label_ref, rows_ref, w_pool_ref, gain_ref, most)
        keys = jnp.dot(normed, w_key_ref[...], preferred_element_type=f32)
        value_ref[at, :] = jnp.dot(normed, w_value_ref[...], preferred_element_type=f32).astype(bf16)
        key_ref[:, at] = jnp.transpose(keys).astype(bf16)


def attend_kernel(factor_ref, query_ref, key_a_ref, value_a_ref, key_b_ref, value_b_ref, out_ref):
    rows = query_ref.shape[0]
    chunk = value_a_ref.shape[0] // 2
    chunks = [(k, v, slice(c, c + chunk)) for k, v in ((key_a_ref, value_a_ref), (key_b_ref, value_b_ref)) for c in (0, chunk)]
    ones = jnp.ones((chunk, 128), bf16)
    stats, scores = [], []
    for g in range(2):
        scaled = jnp.concatenate(
            [query_ref[:, h * 128:(h + 1) * 128].astype(f32) * factor_ref[h] for h in range(4 * g, 4 * g + 4)], axis=0
        )
        high = scaled.astype(bf16)
        low = (scaled - high.astype(f32)).astype(bf16)
        query = jnp.concatenate([high, low], axis=1)
        own = slice(g * 128, (g + 1) * 128)
        scores.append(
            [jnp.dot(query, jnp.concatenate([k[own, c]] * 2, axis=0), preferred_element_type=f32) for k, v, c in chunks]
        )
    for g in range(2):
        own = slice(g * 128, (g + 1) * 128)
        tops = [jnp.max(score, axis=1, keepdims=True) for score in scores[g]]
        top = functools.reduce(jnp.maximum, tops)
        both = 0.0
        for score, (k, v, c) in zip(scores[g], chunks):
            weight = jnp.exp2(score - top).astype(bf16)
            both += jnp.dot(weight, jnp.concatenate([v[c, own], ones], axis=1), preferred_element_type=f32)
        norm = both[:, 128:]
        attn = (both[:, :128] / norm).astype(bf16)
        level = top + jnp.log2(norm)
        for r in range(4):
            h = 4 * g + r
            out_ref[:, h * 128:(h + 1) * 128] = attn[r * rows:(r + 1) * rows]
            stats.append(level[r * rows:(r + 1) * rows])
    lanes = lax.broadcasted_iota(i32, (rows, 128), 1)
    level = jnp.zeros((rows, 128), f32)
    for h in range(8):
        level = jnp.where(lanes == h, stats[h], level)
    high = level.astype(bf16)
    rest = level - high.astype(f32)
    middle = rest.astype(bf16)
    low = (rest - middle.astype(f32)).astype(bf16)
    out_ref[:, 1024:1152] = high
    out_ref[:, 1152:1280] = middle
    out_ref[:, 1280:1408] = low


def merge_kernel(a_ref, b_ref, c_ref, d_ref, coarse_ref, w_out_ref, out_ref):
    refs = (a_ref, b_ref, c_ref, d_ref)
    levels = [r[:, 1024:1152].astype(f32) + (r[:, 1152:1280].astype(f32) + r[:, 1280:1408].astype(f32)) for r in refs]
    top = jnp.maximum(jnp.maximum(levels[0], levels[1]), jnp.maximum(levels[2], levels[3]))
    shares = [jnp.exp2(level - top) for level in levels]
    whole = shares[0] + shares[1] + shares[2] + shares[3]
    shares = [share / whole for share in shares]
    pieces = []
    for h in range(8):
        at = slice(h * 128, (h + 1) * 128)
        pieces.append(sum(r[:, at].astype(f32) * s[:, h:h + 1] for r, s in zip(refs, shares)))
    attn = jnp.concatenate(pieces, axis=1).astype(bf16)
    out_ref[...] = (coarse_ref[...] + jnp.dot(attn, w_out_ref[...], preferred_element_type=f32)).astype(bf16)


def body(fine_state, send_index, edge_src, edge_dst, cell_slot, slot_parent, w_src, w_dst, msg_bias, w_msg, w_upd,
         w_pool, norm_gain, w_query, w_key, w_value, w_out, head_scale):
    groups, devices = lax.axis_size("grp"), lax.axis_size("cur")
    smem = pl.BlockSpec(memory_space=pltpu.SMEM)
    vmem = pl.BlockSpec(memory_space=pltpu.VMEM)
    every = groups * devices
    both = ("grp", "cur")
    before = lax.ppermute(fine_state[send_index[0, 0]], both, [(i, (i + 1) % every) for i in range(every)])
    after = lax.ppermute(fine_state[send_index[0, 1]], both, [(i, (i - 1) % every) for i in range(every)])
    slots = slot_parent.shape[1]
    par_dev = slots - 1
    parents = jnp.full((256,), -64, i32).at[:slots].set(slot_parent[0])
    tags = jnp.zeros((SLOT_ROWS, 256), i32).at[slots].set(parents >> 6).at[slots + 1].set(parents & 63).astype(bf16)
    fine_out, part = fine_pass(fine_state, before, after, edge_src[0], edge_dst[0], cell_slot, tags,
                               w_src, w_dst, msg_bias, w_msg, w_upd)
    blocks = gather_group(part)
    labels = (blocks[:, slots, :SLOT_ROWS].astype(i32) * 64 + blocks[:, slots + 1, :SLOT_ROWS].astype(i32)).reshape(1, -1)
    rows = blocks.reshape(-1, 256)
    gain = norm_gain.reshape(1, -1)
    width = w_query.shape[1]
    params = pltpu.CompilerParams(vmem_limit_bytes=56 << 20)
    coarse, query = pl.pallas_call(
        query_kernel,
        out_shape=(jax.ShapeDtypeStruct((par_dev, width), f32), jax.ShapeDtypeStruct((par_dev, width), bf16)),
        in_specs=[smem] + [vmem] * 5,
        out_specs=(vmem, vmem),
        compiler_params=params,
        name="own_query",
    )((lax.axis_index("cur") * par_dev)[None], labels, rows, w_pool, gain, w_query)
    asked = {by: lax.ppermute(query, "grp", [(i, (i + by) % groups) for i in range(groups)]) for by in (2, 1, 3)}
    asked[0] = query
    known = par_dev * devices // 2
    step = 512
    whole = lambda *shape: pl.BlockSpec(shape, lambda i: (0,) * len(shape))
    keys, values = pl.pallas_call(
        key_kernel,
        out_shape=(jax.ShapeDtypeStruct((256, known), bf16), jax.ShapeDtypeStruct((known, 256), bf16)),
        grid=(known // step,),
        in_specs=[smem, whole(*labels.shape), whole(*rows.shape), whole(*w_pool.shape), whole(*gain.shape),
                  whole(*w_key.shape), whole(*w_value.shape)],
        out_specs=(pl.BlockSpec((256, step), lambda i: (0, i)), pl.BlockSpec((step, 256), lambda i: (i, 0))),
        compiler_params=params,
        name="group_keys",
    )(((lax.axis_index("cur") & 1) * known)[None], labels, rows, w_pool, gain, w_key, w_value)
    swap = [(i, i ^ 1) for i in range(devices)]
    twin_keys, twin_values = lax.ppermute(keys, "cur", swap), lax.ppermute(values, "cur", swap)
    factor = head_scale * (math.log2(math.e) / math.sqrt(128.0))
    found = []
    for by in (2, 1, 3, 0):
        piece = pl.pallas_call(
            attend_kernel,
            out_shape=jax.ShapeDtypeStruct((par_dev, width + 384), bf16),
            in_specs=[smem] + [vmem] * 5,
            out_specs=vmem,
            compiler_params=params,
            name="attend",
        )(factor, asked[by], keys, values, twin_keys, twin_values)
        if by:
            piece = lax.ppermute(piece, "grp", [(i, (i - by) % groups) for i in range(groups)])
        found.append(piece)
    coarse_out = pl.pallas_call(
        merge_kernel,
        out_shape=jax.ShapeDtypeStruct((par_dev, width), bf16),
        in_specs=[vmem] * 6,
        out_specs=vmem,
        compiler_params=params,
        name="merge",
    )(*found, coarse, w_out)
    return fine_out, coarse_out


def solution(mesh):
    line = P(("grp", "cur"), None)
    in_specs = (line, P(("grp", "cur"), None, None), line, line, P(("grp", "cur")), line) + (P(),) * 12
    return jax.shard_map(body, mesh=mesh, in_specs=in_specs, out_specs=(line, line), check_vma=False)
```

```python
import functools
import math
import jax, jax.numpy as jnp
from jax import lax
from jax.experimental import pallas as pl
from jax.experimental.pallas import tpu as pltpu
from jax.sharding import PartitionSpec as P

TILE = 256
WINDOW = 128
TOGETHER = 4
TARGET_SHIFT = 13
NO_TARGET = 6144
SLOT_ROWS = 104
bf16, f32, i32 = jnp.bfloat16, jnp.float32, jnp.int32


def sort_kernel(source_ref, target_ref, rows_ref, targets_ref, key):
    given = source_ref.shape[0]
    fill = jnp.full((8, 128), NO_TARGET << TARGET_SHIFT, i32)
    held = [(target_ref[v] << TARGET_SHIFT) | source_ref[v] if v < given else fill for v in range(64)]
    for phase in range(1, 6):
        for bit in range(phase - 1, -1, -1):
            for v in range(64):
                if not v >> bit & 1:
                    w = v | 1 << bit
                    small, large = jnp.minimum(held[v], held[w]), jnp.maximum(held[v], held[w])
                    held[v], held[w] = (large, small) if v >> phase & 1 else (small, large)
    for v in range(64):
        key[v >> 3, v & 7] = held[v]
    row = lax.broadcasted_iota(i32, (8, 128), 0)
    lane = lax.broadcasted_iota(i32, (8, 128), 1)

    def bit_of(bit):
        if bit == 16:
            return jnp.zeros((8, 128), i32)
        return (row >> (bit - 6) & 1) if bit < 9 else (lane >> (bit - 9) & 1)

    for phase in range(6, 17):
        flip = bit_of(phase) if phase == 6 else bit_of(phase) ^ bit_of(phase - 1)

        def across(g, carry):
            held = key[pl.ds(2 * g, 2)].reshape(16, 8, 128) ^ (-flip)[None]
            for bit in range(phase - 1, 5, -1):
                axis, by, size = (1, 1 << (bit - 6), 8) if bit < 9 else (2, 1 << (bit - 9), 128)
                upper = (bit_of(bit) == 1)[None]
                if 2 * by == size:
                    other = pltpu.roll(held, by, axis)
                else:
                    other = jnp.where(upper, pltpu.roll(held, by, axis), pltpu.roll(held, size - by, axis))
                held = jnp.where(upper, jnp.maximum(held, other), jnp.minimum(held, other))
            key[pl.ds(2 * g, 2)] = held.reshape(2, 8, 8, 128)
            return carry

        lax.fori_loop(0, 4, across, 0, unroll=4)

        def merge(held):
            for bit in (2, 1, 0):
                pairs = held.reshape(4 >> bit, 2, 1 << bit, 8, 128)
                held = jnp.stack(
                    [jnp.minimum(pairs[:, 0], pairs[:, 1]), jnp.maximum(pairs[:, 0], pairs[:, 1])], axis=1
                ).reshape(8, 8, 128)
            return held

        def high(g, carry):
            key[:, g] = merge(key[:, g])
            return carry

        def low(g, carry):
            key[g] = merge(key[g])
            return carry

        lax.fori_loop(0, 8, high, 0, unroll=8)
        lax.fori_loop(0, 8, low, 0, unroll=8)

    flat = key.reshape(512, 128)
    half = rows_ref.shape[1] // 2
    for part in range(4):
        piece = jnp.concatenate([flat[pl.ds(s, 64, stride=8), :] for s in (2 * part, 2 * part + 1)], axis=0)
        piece = jnp.transpose(piece)[:half]
        at = (part % 2, pl.ds(part // 2, half, stride=2), slice(None))
        rows_ref[at] = (piece & ((1 << TARGET_SHIFT) - 1)) * 2
        targets_ref[at] = piece >> TARGET_SHIFT


def sorted_edges(source, target):
    edges = source.shape[0]
    shape = jax.ShapeDtypeStruct((2, edges // TILE, 128), i32)
    return pl.pallas_call(
        sort_kernel,
        out_shape=(shape, shape),
        scratch_shapes=[pltpu.VMEM((8, 8, 8, 128), i32)],
        compiler_params=pltpu.CompilerParams(vmem_limit_bytes=24 << 20),
        name="sort_edges",
    )(source.reshape(-1, 8, 128), target.reshape(-1, 8, 128))


def fine_kernel(rows_ref, meta_ref, local_ref, slot_ref, tag_ref, own_ref, before_ref, after_ref, w_src_ref, w_dst_ref,
                bias_ref, w_msg_ref, w_upd_ref, out_ref, part_ref, table, dst, total, count, got_a, got_b):
    blocks = own_ref.shape[0] // TILE
    tiles_most = local_ref.shape[1]

    def put_table(places, groups):
        projs = [jnp.dot(rows, w_src_ref[...], preferred_element_type=f32).astype(bf16).astype(f32) for rows in groups]
        for place, proj in zip(places, projs):
            proj = proj + bias_ref[...]
            table[pl.ds(2 * place, TILE, stride=2), :] = proj[:, :128]
            table[pl.ds(2 * place + 1, TILE, stride=2), :] = proj[:, 128:]

    def project(j, carry):
        places = [pl.multiple_of((j * TOGETHER + n) * TILE, TILE) for n in range(TOGETHER)]
        groups = [own_ref[pl.ds(at, TILE), :] for at in places]
        put_table(places, groups)
        mine = [jnp.dot(own, w_dst_ref[...], preferred_element_type=f32).astype(bf16) for own in groups]
        for at, proj in zip(places, mine):
            dst[pl.ds(at, TILE), :] = proj
            total[pl.ds(at, TILE), :] = jnp.zeros((TILE, 256), f32)
            count[pl.ds(at, TILE), :] = jnp.zeros((TILE, 128), f32)
        return carry

    lax.fori_loop(0, blocks // TOGETHER, project, 0)
    put_table((blocks * TILE, blocks * TILE + TILE), (before_ref[...], after_ref[...]))

    place = lax.broadcasted_iota(i32, (WINDOW, TILE), 0).astype(f32).astype(bf16)
    one, zero = jnp.ones((WINDOW, TILE), bf16), jnp.zeros((WINDOW, TILE), bf16)
    ones = jnp.ones((TILE, 128), bf16)

    def fetch(base, first, last, got):
        for i in range(first, last):
            place = i % TILE // 128 * (tiles_most * 128) + i // TILE * 128 + i % 128
            got[2 * i:2 * i + 2, :] = table[pl.ds(rows_ref[base + place], 2), :]

    def tile_steps(tile, n, got, start):
        state = {}

        def first():
            state["at"] = at = pl.multiple_of(start, 16)
            local = jnp.concatenate([local_ref[k, pl.ds(tile, 1), :] for k in range(2)], axis=1)
            local = jnp.minimum(local - at, WINDOW).astype(f32).astype(bf16)
            state["hot"] = jnp.where(place == local, one, zero)
            state["own"] = lax.dot_general(
                state["hot"], dst[pl.ds(at, WINDOW), :], (((0,), (0,)), ((), ())), preferred_element_type=f32
            )

        def second():
            sent = [got[pl.ds(2 * TILE * n + k, TILE, stride=2), :] for k in range(2)]
            half = 0.5 * (state["own"] + jnp.concatenate(sent, axis=1))
            state["hidden"] = (half + half * jnp.tanh(half)).astype(bf16)

        def third():
            at = pl.ds(state["at"], WINDOW)
            total[at, :] += jnp.dot(state["hot"], state["hidden"], preferred_element_type=f32)
            count[at, :] += jnp.dot(state["hot"], ones, preferred_element_type=f32)

        return first, second, third

    def advance(tile, got, ahead, got_ahead):
        base = jnp.minimum(ahead, tiles_most - TOGETHER) * 128
        tiles = [tile_steps(tile + n, n, got, meta_ref[tile + n]) for n in range(TOGETHER)]
        steps = [run for steps in zip(*tiles) for run in steps]
        rows = TOGETHER * TILE
        for i, run in enumerate(steps):
            fetch(base, rows * i // len(steps), rows * (i + 1) // len(steps), got_ahead)
            run()

    def step(j, carry):
        tile = 2 * TOGETHER * j
        advance(tile, got_a, tile + TOGETHER, got_b)
        advance(tile + TOGETHER, got_b, tile + 2 * TOGETHER, got_a)
        return carry

    fetch(0, 0, TOGETHER * TILE, got_a)
    lax.fori_loop(0, meta_ref[2 * tiles_most], step, 0)

    def rest(tile, carry):
        def window(w, carry):
            fetch(tile * 128, 0, TILE, got_a)
            for run in tile_steps(tile, 0, got_a, jnp.minimum(meta_ref[tile] + w * WINDOW, blocks * TILE - WINDOW)):
                run()
            return carry

        return lax.fori_loop(1, meta_ref[tiles_most + tile], window, carry)

    lax.fori_loop(0, tiles_most, rest, 0)

    slots = lax.broadcasted_iota(i32, (SLOT_ROWS, TILE), 0)

    def finish(j, parts):
        group = [j * TOGETHER + n for n in range(TOGETHER)]
        spots = [pl.ds(pl.multiple_of(b * TILE, TILE), TILE) for b in group]
        w_msg = w_msg_ref[...]
        highs, lows = [], []
        for at in spots:
            scale = 1.0 / jnp.maximum(count[at, :], 1.0)
            mean = total[at, :] * jnp.concatenate([scale, scale], axis=1)
            highs.append(mean.astype(bf16))
            lows.append((mean - highs[-1].astype(f32)).astype(bf16))
        aggs = [
            jnp.dot(high, w_msg, preferred_element_type=f32) + jnp.dot(low, w_msg, preferred_element_type=f32)
            for high, low in zip(highs, lows)
        ]
        updates = [jnp.dot(agg.astype(bf16), w_upd_ref[...], preferred_element_type=f32) for agg in aggs]
        for b, at, update in zip(group, spots, updates):
            new = (own_ref[at, :].astype(f32) + update).astype(bf16)
            out_ref[at, :] = new
            hot = (slots == slot_ref[b]).astype(f32).astype(bf16)
            parts += jnp.dot(hot, new, preferred_element_type=f32)
        return parts

    parts = lax.fori_loop(0, blocks // TOGETHER, finish, tag_ref[...].astype(f32))
    part_ref[...] = parts.astype(bf16)


def fine_pass(own, before, after, source, target, cell_slot, tags, w_src, w_dst, bias, w_msg, w_upd):
    cells = own.shape[0]
    blocks = cells // TILE
    tiles = source.shape[0] // TILE
    rows, targets = sorted_edges(source, target)
    start = jnp.minimum(targets[0, :, 0] & -16, cells - WINDOW)
    last = jnp.max(jnp.where(targets < cells, targets, -1), axis=(0, 2))
    windows = jnp.maximum(last + WINDOW - start, 0) // WINDOW
    pairs = (jnp.sum((last >= 0).astype(i32)) + (2 * TOGETHER - 1)) // (2 * TOGETHER)
    meta = jnp.concatenate([start, windows, pairs[None]])
    smem = pl.BlockSpec(memory_space=pltpu.SMEM)
    vmem = pl.BlockSpec(memory_space=pltpu.VMEM)
    return pl.pallas_call(
        fine_kernel,
        out_shape=(jax.ShapeDtypeStruct(own.shape, bf16), jax.ShapeDtypeStruct((SLOT_ROWS, 256), bf16)),
        in_specs=[smem, smem] + [vmem] * 11,
        out_specs=(vmem, vmem),
        scratch_shapes=[
            pltpu.VMEM((2 * (cells + 2 * TILE), 128), f32),
            pltpu.VMEM((cells, 256), bf16),
            pltpu.VMEM((cells, 256), f32),
            pltpu.VMEM((cells, 128), f32),
            pltpu.VMEM((2 * TOGETHER * TILE, 128), f32),
            pltpu.VMEM((2 * TOGETHER * TILE, 128), f32),
        ],
        compiler_params=pltpu.CompilerParams(vmem_limit_bytes=58 << 20),
        name="fine_cells",
    )(rows.reshape(-1), meta, targets, cell_slot.reshape(blocks, 1, TILE), tags, own, before, after, w_src, w_dst,
      bias.reshape(1, -1), w_msg, w_upd)


def moved(value, axis, pairs):
    return lax.ppermute(value, axis, pairs)


def ring_gather(value, move):
    return jnp.concatenate([value] + [move(value, by) for by in (1, 3, 2)], axis=0)


def gather_group(part):
    devices = lax.axis_size("cur")

    def along_z(value, by):
        return lax.ppermute(value, "cur", [(i, i // 8 * 8 + (i + 2 * by) % 8) for i in range(devices)])

    def along_x(value, by):
        return lax.ppermute(value, "cur", [(i, (i + 8 * by) % devices) for i in range(devices)])

    rows = ring_gather(part[None], along_z)
    rows = ring_gather(rows, along_x)
    return jnp.concatenate([rows, lax.ppermute(rows, "cur", [(i, i ^ 1) for i in range(devices)])], axis=0)


def normed_parents(firsts, label_ref, rows_ref, w_pool_ref, gain_ref, parents):
    shape = (parents, rows_ref.shape[0])
    ids = lax.broadcasted_iota(i32, shape, 0).astype(f32).astype(bf16)
    one, zero = jnp.ones(shape, bf16), jnp.zeros(shape, bf16)
    labels = [jnp.clip(label_ref[...] - first, -1, 256).astype(f32).astype(bf16) for first in firsts]
    sums = [jnp.dot(jnp.where(ids == label, one, zero), rows_ref[...], preferred_element_type=f32) for label in labels]
    means = [(total * (1.0 / 64.0)).astype(bf16) for total in sums]
    coarse = [jnp.dot(mean, w_pool_ref[...], preferred_element_type=f32) for mean in means]
    inverse = [lax.rsqrt(jnp.mean(rows * rows, axis=1, keepdims=True) + 1e-06) for rows in coarse]
    return coarse, [(rows * scale * gain_ref[...]).astype(bf16) for rows, scale in zip(coarse, inverse)]


def query_kernel(first_ref, label_ref, rows_ref, w_pool_ref, gain_ref, w_query_ref, coarse_ref, query_ref):
    coarse, normed = normed_parents([first_ref[0]], label_ref, rows_ref, w_pool_ref, gain_ref, query_ref.shape[0])
    coarse_ref[...] = coarse[0]
    query_ref[...] = jnp.dot(normed[0], w_query_ref[...], preferred_element_type=f32).astype(bf16)


def key_kernel(first_ref, label_ref, rows_ref, w_pool_ref, gain_ref, w_key_ref, w_value_ref, key_ref, value_ref):
    most = 256
    parts = value_ref.shape[0] // most
    firsts = [first_ref[0] + pl.program_id(0) * value_ref.shape[0] + part * most for part in range(parts)]
    normed = normed_parents(firsts, label_ref, rows_ref, w_pool_ref, gain_ref, most)[1]
    keys = [jnp.dot(rows, w_key_ref[...], preferred_element_type=f32) for rows in normed]
    values = [jnp.dot(rows, w_value_ref[...], preferred_element_type=f32) for rows in normed]
    for part in range(parts):
        at = slice(part * most, (part + 1) * most)
        value_ref[at, :] = values[part].astype(bf16)
        key_ref[:, at] = jnp.transpose(keys[part]).astype(bf16)


def halo_kernel(index_ref, own_ref, before_ref, after_ref):
    lane = lax.broadcasted_iota(i32, (128, 128), 1)
    wanted = [jnp.transpose(jnp.broadcast_to(index_ref[r:r + 1, :], (128, 128))) - lane for r in range(4)]
    step = 1024
    found = 0.0
    for start in range(0, own_ref.shape[0], step):
        hot = jnp.concatenate(
            [jnp.concatenate([(w == start + t).astype(f32).astype(bf16) for t in range(0, step, 128)], axis=1) for w in wanted],
            axis=0,
        )
        found += jnp.dot(hot, own_ref[start:start + step, :], preferred_element_type=f32)
    half = before_ref.shape[0]
    before_ref[...] = found[:half].astype(bf16)
    after_ref[...] = found[half:].astype(bf16)


def attend_kernel(factor_ref, key_a_ref, value_a_ref, key_b_ref, value_b_ref, *refs):
    query_refs, out_refs = refs[:len(refs) // 2], refs[len(refs) // 2:]
    rows = query_refs[0].shape[0]
    chunk = value_a_ref.shape[0] // 2
    chunks = [(k, v, slice(c, c + chunk)) for k, v in ((key_a_ref, value_a_ref), (key_b_ref, value_b_ref)) for c in (0, chunk)]
    ones = jnp.ones((chunk, 128), bf16)
    scores = []
    for g in range(2):
        scaled = jnp.concatenate(
            [ref[:, h * 128:(h + 1) * 128].astype(f32) * factor_ref[h] for ref in query_refs for h in range(4 * g, 4 * g + 4)],
            axis=0,
        )
        high = scaled.astype(bf16)
        low = (scaled - high.astype(f32)).astype(bf16)
        query = jnp.concatenate([high, low], axis=1)
        own = slice(g * 128, (g + 1) * 128)
        scores.append(
            [jnp.dot(query, jnp.concatenate([k[own, c]] * 2, axis=0), preferred_element_type=f32) for k, v, c in chunks]
        )
    levels = [jnp.zeros((rows, 128), f32) for ref in out_refs]
    lanes = lax.broadcasted_iota(i32, (rows, 128), 1)
    for g in range(2):
        own = slice(g * 128, (g + 1) * 128)
        top = functools.reduce(jnp.maximum, [jnp.max(score, axis=1, keepdims=True) for score in scores[g]])
        both = 0.0
        for score, (k, v, c) in zip(scores[g], chunks):
            weight = jnp.exp2(score - top).astype(bf16)
            both += jnp.dot(weight, jnp.concatenate([v[c, own], ones], axis=1), preferred_element_type=f32)
        norm = both[:, 128:]
        attn = (both[:, :128] / norm).astype(bf16)
        level = top + jnp.log2(norm)
        for n, out_ref in enumerate(out_refs):
            for r in range(4):
                h = 4 * g + r
                at = slice((4 * n + r) * rows, (4 * n + r + 1) * rows)
                out_ref[:, h * 128:(h + 1) * 128] = attn[at]
                levels[n] = jnp.where(lanes == h, level[at], levels[n])
    for level, out_ref in zip(levels, out_refs):
        high = level.astype(bf16)
        rest = level - high.astype(f32)
        middle = rest.astype(bf16)
        out_ref[:, 1024:1152] = high
        out_ref[:, 1152:1280] = middle
        out_ref[:, 1280:1408] = (rest - middle.astype(f32)).astype(bf16)


def merge_kernel(a_ref, b_ref, c_ref, d_ref, coarse_ref, w_out_ref, out_ref):
    refs = (a_ref, b_ref, c_ref, d_ref)
    levels = [r[:, 1024:1152].astype(f32) + (r[:, 1152:1280].astype(f32) + r[:, 1280:1408].astype(f32)) for r in refs]
    top = jnp.maximum(jnp.maximum(levels[0], levels[1]), jnp.maximum(levels[2], levels[3]))
    shares = [jnp.exp2(level - top) for level in levels]
    whole = shares[0] + shares[1] + shares[2] + shares[3]
    shares = [share / whole for share in shares]
    pieces = []
    for h in range(8):
        at = slice(h * 128, (h + 1) * 128)
        pieces.append(sum(r[:, at].astype(f32) * s[:, h:h + 1] for r, s in zip(refs, shares)))
    attn = jnp.concatenate(pieces, axis=1).astype(bf16)
    out_ref[...] = (coarse_ref[...] + jnp.dot(attn, w_out_ref[...], preferred_element_type=f32)).astype(bf16)


def body(fine_state, send_index, edge_src, edge_dst, cell_slot, slot_parent, w_src, w_dst, msg_bias, w_msg, w_upd,
         w_pool, norm_gain, w_query, w_key, w_value, w_out, head_scale):
    groups, devices = lax.axis_size("grp"), lax.axis_size("cur")
    smem = pl.BlockSpec(memory_space=pltpu.SMEM)
    vmem = pl.BlockSpec(memory_space=pltpu.VMEM)
    every = groups * devices
    both = ("grp", "cur")
    params = pltpu.CompilerParams(vmem_limit_bytes=56 << 20)
    halo = send_index.shape[2]
    to_next, to_prev = pl.pallas_call(
        halo_kernel,
        out_shape=[jax.ShapeDtypeStruct((halo, fine_state.shape[1]), bf16)] * 2,
        in_specs=[vmem] * 2,
        out_specs=[vmem] * 2,
        compiler_params=params,
        name="halo_cells",
    )(send_index.reshape(-1, 128), fine_state)
    before = lax.ppermute(to_next, both, [(i, (i + 1) % every) for i in range(every)])
    after = lax.ppermute(to_prev, both, [(i, (i - 1) % every) for i in range(every)])
    slots = slot_parent.shape[1]
    par_dev = slots - 1
    parents = jnp.full((256,), -64, i32).at[:slots].set(slot_parent[0])
    tags = jnp.zeros((SLOT_ROWS, 256), i32).at[slots].set(parents >> 6).at[slots + 1].set(parents & 63).astype(bf16)
    fine_out, part = fine_pass(fine_state, before, after, edge_src[0], edge_dst[0], cell_slot, tags,
                               w_src, w_dst, msg_bias, w_msg, w_upd)
    blocks = gather_group(part)
    labels = (blocks[:, slots, :SLOT_ROWS].astype(i32) * 64 + blocks[:, slots + 1, :SLOT_ROWS].astype(i32)).reshape(1, -1)
    rows = blocks.reshape(-1, 256)
    gain = norm_gain.reshape(1, -1)
    width = w_query.shape[1]
    coarse, query = pl.pallas_call(
        query_kernel,
        out_shape=(jax.ShapeDtypeStruct((par_dev, width), f32), jax.ShapeDtypeStruct((par_dev, width), bf16)),
        in_specs=[smem] + [vmem] * 5,
        out_specs=(vmem, vmem),
        compiler_params=params,
        name="own_query",
    )((lax.axis_index("cur") * par_dev)[None], labels, rows, w_pool, gain, w_query)
    query, rows = lax.optimization_barrier((query, rows))
    asked = {by: lax.ppermute(query, "grp", [(i, (i + by) % groups) for i in range(groups)]) for by in (2, 1, 3)}
    asked[0] = query
    known = par_dev * devices // 2
    step = known
    whole = lambda *shape: pl.BlockSpec(shape, lambda i: (0,) * len(shape))
    keys, values = pl.pallas_call(
        key_kernel,
        out_shape=(jax.ShapeDtypeStruct((256, known), bf16), jax.ShapeDtypeStruct((known, 256), bf16)),
        grid=(known // step,),
        in_specs=[smem, whole(*labels.shape), whole(*rows.shape), whole(*w_pool.shape), whole(*gain.shape),
                  whole(*w_key.shape), whole(*w_value.shape)],
        out_specs=(pl.BlockSpec((256, step), lambda i: (0, i)), pl.BlockSpec((step, 256), lambda i: (i, 0))),
        compiler_params=params,
        name="group_keys",
    )(((lax.axis_index("cur") & 1) * known)[None], labels, rows, w_pool, gain, w_key, w_value)
    swap = [(i, i ^ 1) for i in range(devices)]
    twin_keys, twin_values = lax.ppermute(keys, "cur", swap), lax.ppermute(values, "cur", swap)
    factor = head_scale * (math.log2(math.e) / math.sqrt(128.0))
    found = []
    for shifts in ((2,), (1, 3), (0,)):
        pieces = pl.pallas_call(
            attend_kernel,
            out_shape=[jax.ShapeDtypeStruct((par_dev, width + 384), bf16) for by in shifts],
            in_specs=[smem] + [vmem] * (4 + len(shifts)),
            out_specs=[vmem for by in shifts],
            compiler_params=params,
            name="attend",
        )(factor, keys, values, twin_keys, twin_values, *[asked[by] for by in shifts])
        for by, piece in zip(shifts, pieces):
            found.append(lax.ppermute(piece, "grp", [(i, (i - by) % groups) for i in range(groups)]) if by else piece)
    coarse_out = pl.pallas_call(
        merge_kernel,
        out_shape=jax.ShapeDtypeStruct((par_dev, width), bf16),
        in_specs=[vmem] * 6,
        out_specs=vmem,
        compiler_params=params,
        name="merge",
    )(*found, coarse, w_out)
    return fine_out, coarse_out


def solution(mesh):
    line = P(("grp", "cur"), None)
    in_specs = (line, P(("grp", "cur"), None, None), line, line, P(("grp", "cur")), line) + (P(),) * 12
    return jax.shard_map(body, mesh=mesh, in_specs=in_specs, out_specs=(line, line), check_vma=False)
```

```python
import functools
import math
import jax, jax.numpy as jnp
from jax import lax
from jax.experimental import pallas as pl
from jax.experimental.pallas import tpu as pltpu
from jax.sharding import PartitionSpec as P

TILE = 256
WINDOW = 128
TOGETHER = 4
TARGET_SHIFT = 13
NO_TARGET = 6144
SLOT_ROWS = 104
SLOTS = 97
bf16, f32, i32 = jnp.bfloat16, jnp.float32, jnp.int32


def sort_kernel(source_ref, target_ref, rows_ref, targets_ref, key):
    given = source_ref.shape[0]
    fill = jnp.full((8, 128), NO_TARGET << TARGET_SHIFT, i32)
    held = [(target_ref[v] << TARGET_SHIFT) | source_ref[v] if v < given else fill for v in range(64)]
    for phase in range(1, 6):
        for bit in range(phase - 1, -1, -1):
            for v in range(64):
                if not v >> bit & 1:
                    w = v | 1 << bit
                    small, large = jnp.minimum(held[v], held[w]), jnp.maximum(held[v], held[w])
                    held[v], held[w] = (large, small) if v >> phase & 1 else (small, large)
    for v in range(64):
        key[v >> 3, v & 7] = held[v]
    row = lax.broadcasted_iota(i32, (8, 128), 0)
    lane = lax.broadcasted_iota(i32, (8, 128), 1)

    def bit_of(bit):
        if bit == 16:
            return jnp.zeros((8, 128), i32)
        return (row >> (bit - 6) & 1) if bit < 9 else (lane >> (bit - 9) & 1)

    for phase in range(6, 17):
        flip = bit_of(phase) if phase == 6 else bit_of(phase) ^ bit_of(phase - 1)

        def across(g, carry):
            held = key[pl.ds(2 * g, 2)].reshape(16, 8, 128) ^ (-flip)[None]
            for bit in range(phase - 1, 5, -1):
                axis, by, size = (1, 1 << (bit - 6), 8) if bit < 9 else (2, 1 << (bit - 9), 128)
                upper = (bit_of(bit) == 1)[None]
                if 2 * by == size:
                    other = pltpu.roll(held, by, axis)
                else:
                    other = jnp.where(upper, pltpu.roll(held, by, axis), pltpu.roll(held, size - by, axis))
                held = jnp.where(upper, jnp.maximum(held, other), jnp.minimum(held, other))
            key[pl.ds(2 * g, 2)] = held.reshape(2, 8, 8, 128)
            return carry

        lax.fori_loop(0, 4, across, 0, unroll=4)

        def merge(held):
            for bit in (2, 1, 0):
                pairs = held.reshape(4 >> bit, 2, 1 << bit, 8, 128)
                held = jnp.stack(
                    [jnp.minimum(pairs[:, 0], pairs[:, 1]), jnp.maximum(pairs[:, 0], pairs[:, 1])], axis=1
                ).reshape(8, 8, 128)
            return held

        def high(g, carry):
            key[:, g] = merge(key[:, g])
            return carry

        def low(g, carry):
            key[g] = merge(key[g])
            return carry

        lax.fori_loop(0, 8, high, 0, unroll=8)
        lax.fori_loop(0, 8, low, 0, unroll=8)

    flat = key.reshape(512, 128)
    half = rows_ref.shape[1] // 2
    for part in range(4):
        piece = jnp.concatenate([flat[pl.ds(s, 64, stride=8), :] for s in (2 * part, 2 * part + 1)], axis=0)
        piece = jnp.transpose(piece)[:half]
        at = (part % 2, pl.ds(part // 2, half, stride=2), slice(None))
        rows_ref[at] = (piece & ((1 << TARGET_SHIFT) - 1)) * 2
        targets_ref[at] = piece >> TARGET_SHIFT


def sorted_edges(source, target):
    edges = source.shape[0]
    shape = jax.ShapeDtypeStruct((2, edges // TILE, 128), i32)
    return pl.pallas_call(
        sort_kernel,
        out_shape=(shape, shape),
        scratch_shapes=[pltpu.VMEM((8, 8, 8, 128), i32)],
        compiler_params=pltpu.CompilerParams(vmem_limit_bytes=24 << 20),
        name="sort_edges",
    )(source.reshape(-1, 8, 128), target.reshape(-1, 8, 128))


def fine_kernel(rows_ref, start_ref, windows_ref, pairs_ref, local_ref, slot_ref, parent_ref, own_ref, before_ref, after_ref, w_src_ref, w_dst_ref,
                bias_ref, w_msg_ref, w_upd_ref, out_ref, part_ref, table, dst, total, count, got_a, got_b):
    blocks = own_ref.shape[0] // TILE
    tiles_most = local_ref.shape[1]

    def put_table(places, groups):
        projs = [jnp.dot(rows, w_src_ref[...], preferred_element_type=f32).astype(bf16).astype(f32) for rows in groups]
        for place, proj in zip(places, projs):
            proj = proj + bias_ref[...]
            table[pl.ds(2 * place, TILE, stride=2), :] = proj[:, :128]
            table[pl.ds(2 * place + 1, TILE, stride=2), :] = proj[:, 128:]

    def project(j, carry):
        places = [pl.multiple_of((j * TOGETHER + n) * TILE, TILE) for n in range(TOGETHER)]
        groups = [own_ref[pl.ds(at, TILE), :] for at in places]
        put_table(places, groups)
        mine = [jnp.dot(own, w_dst_ref[...], preferred_element_type=f32).astype(bf16) for own in groups]
        for at, proj in zip(places, mine):
            dst[pl.ds(at, TILE), :] = proj
            total[pl.ds(at, TILE), :] = jnp.zeros((TILE, 256), f32)
            count[pl.ds(at, TILE), :] = jnp.zeros((TILE, 128), f32)
        return carry

    lax.fori_loop(0, blocks // TOGETHER, project, 0)
    put_table((blocks * TILE, blocks * TILE + TILE), (before_ref[...], after_ref[...]))

    place = lax.broadcasted_iota(i32, (WINDOW, TILE), 0).astype(f32).astype(bf16)
    one, zero = jnp.ones((WINDOW, TILE), bf16), jnp.zeros((WINDOW, TILE), bf16)
    ones = jnp.ones((TILE, 128), bf16)

    def fetch(base, first, last, got):
        for i in range(first, last):
            place = i % TILE // 128 * (tiles_most * 128) + i // TILE * 128 + i % 128
            got[2 * i:2 * i + 2, :] = table[pl.ds(rows_ref[base + place], 2), :]

    def tile_steps(tile, n, got, start):
        state = {}

        def first():
            state["at"] = at = pl.multiple_of(start, 16)
            local = jnp.concatenate([local_ref[k, pl.ds(tile, 1), :] for k in range(2)], axis=1)
            local = jnp.minimum(local - at, WINDOW).astype(f32).astype(bf16)
            state["hot"] = jnp.where(place == local, one, zero)
            state["own"] = lax.dot_general(
                state["hot"], dst[pl.ds(at, WINDOW), :], (((0,), (0,)), ((), ())), preferred_element_type=f32
            )

        def second():
            sent = [got[pl.ds(2 * TILE * n + k, TILE, stride=2), :] for k in range(2)]
            half = 0.5 * (state["own"] + jnp.concatenate(sent, axis=1))
            state["hidden"] = (half + half * jnp.tanh(half)).astype(bf16)

        def third():
            at = pl.ds(state["at"], WINDOW)
            total[at, :] += jnp.dot(state["hot"], state["hidden"], preferred_element_type=f32)
            count[at, :] += jnp.dot(state["hot"], ones, preferred_element_type=f32)

        return first, second, third

    def advance(tile, got, ahead, got_ahead):
        base = jnp.minimum(ahead, tiles_most - TOGETHER) * 128
        tiles = [tile_steps(tile + n, n, got, start_ref[tile + n]) for n in range(TOGETHER)]
        steps = [run for steps in zip(*tiles) for run in steps]
        rows = TOGETHER * TILE
        for i, run in enumerate(steps):
            fetch(base, rows * i // len(steps), rows * (i + 1) // len(steps), got_ahead)
            run()

    def step(j, carry):
        tile = 2 * TOGETHER * j
        advance(tile, got_a, tile + TOGETHER, got_b)
        advance(tile + TOGETHER, got_b, tile + 2 * TOGETHER, got_a)
        return carry

    fetch(0, 0, TOGETHER * TILE, got_a)
    lax.fori_loop(0, pairs_ref[0], step, 0)

    def rest(tile, carry):
        def window(w, carry):
            fetch(tile * 128, 0, TILE, got_a)
            for run in tile_steps(tile, 0, got_a, jnp.minimum(start_ref[tile] + w * WINDOW, blocks * TILE - WINDOW)):
                run()
            return carry

        return lax.fori_loop(1, windows_ref[tile], window, carry)

    lax.fori_loop(0, tiles_most, rest, 0)

    slots = lax.broadcasted_iota(i32, (SLOT_ROWS, TILE), 0)

    row = lax.broadcasted_iota(i32, (SLOT_ROWS, 256), 0)
    high = jnp.where(row == SLOTS, parent_ref[...] >> 6, 0)
    tags = jnp.where(row == SLOTS + 1, parent_ref[...] & 63, high).astype(f32)

    def finish(j, parts):
        group = [j * TOGETHER + n for n in range(TOGETHER)]
        spots = [pl.ds(pl.multiple_of(b * TILE, TILE), TILE) for b in group]
        w_msg = w_msg_ref[...]
        highs, lows = [], []
        for at in spots:
            scale = 1.0 / jnp.maximum(count[at, :], 1.0)
            mean = total[at, :] * jnp.concatenate([scale, scale], axis=1)
            highs.append(mean.astype(bf16))
            lows.append((mean - highs[-1].astype(f32)).astype(bf16))
        aggs = [
            jnp.dot(high, w_msg, preferred_element_type=f32) + jnp.dot(low, w_msg, preferred_element_type=f32)
            for high, low in zip(highs, lows)
        ]
        updates = [jnp.dot(agg.astype(bf16), w_upd_ref[...], preferred_element_type=f32) for agg in aggs]
        for b, at, update in zip(group, spots, updates):
            new = (own_ref[at, :].astype(f32) + update).astype(bf16)
            out_ref[at, :] = new
            hot = (slots == slot_ref[b]).astype(f32).astype(bf16)
            parts += jnp.dot(hot, new, preferred_element_type=f32)
        return parts

    parts = lax.fori_loop(0, blocks // TOGETHER, finish, tags)
    part_ref[...] = parts.astype(bf16)


def fine_pass(own, before, after, source, target, cell_slot, parents, w_src, w_dst, bias, w_msg, w_upd):
    cells = own.shape[0]
    blocks = cells // TILE
    tiles = source.shape[0] // TILE
    rows, targets = sorted_edges(source, target)
    start = jnp.minimum(targets[0, :, 0] & -16, cells - WINDOW)
    last = jnp.max(jnp.where(targets < cells, targets, -1), axis=(0, 2))
    windows = jnp.maximum(last + WINDOW - start, 0) // WINDOW
    pairs = (jnp.sum((last >= 0).astype(i32)) + (2 * TOGETHER - 1)) // (2 * TOGETHER)
    smem = pl.BlockSpec(memory_space=pltpu.SMEM)
    vmem = pl.BlockSpec(memory_space=pltpu.VMEM)
    return pl.pallas_call(
        fine_kernel,
        out_shape=(jax.ShapeDtypeStruct(own.shape, bf16), jax.ShapeDtypeStruct((SLOT_ROWS, 256), bf16)),
        in_specs=[smem] * 4 + [vmem] * 11,
        out_specs=(vmem, vmem),
        scratch_shapes=[
            pltpu.VMEM((2 * (cells + 2 * TILE), 128), f32),
            pltpu.VMEM((cells, 256), bf16),
            pltpu.VMEM((cells, 256), f32),
            pltpu.VMEM((cells, 128), f32),
            pltpu.VMEM((2 * TOGETHER * TILE, 128), f32),
            pltpu.VMEM((2 * TOGETHER * TILE, 128), f32),
        ],
        compiler_params=pltpu.CompilerParams(vmem_limit_bytes=58 << 20),
        name="fine_cells",
    )(rows.reshape(-1), start, windows, pairs[None], targets, cell_slot.reshape(blocks, 1, TILE), parents, own, before, after, w_src, w_dst,
      bias.reshape(1, -1), w_msg, w_upd)


def moved(value, axis, pairs):
    return lax.ppermute(value, axis, pairs)


def ring_gather(value, move):
    return jnp.concatenate([value] + [move(value, by) for by in (1, 3, 2)], axis=0)


def gather_group(part):
    devices = lax.axis_size("cur")

    def along_z(value, by):
        return lax.ppermute(value, "cur", [(i, i // 8 * 8 + (i + 2 * by) % 8) for i in range(devices)])

    def along_x(value, by):
        return lax.ppermute(value, "cur", [(i, (i + 8 * by) % devices) for i in range(devices)])

    rows = ring_gather(part[None], along_z)
    rows = ring_gather(rows, along_x)
    return jnp.concatenate([rows, lax.ppermute(rows, "cur", [(i, i ^ 1) for i in range(devices)])], axis=0)


def normed_parents(firsts, label_ref, rows_ref, w_pool_ref, gain_ref, parents):
    shape = (parents, rows_ref.shape[0])
    ids = lax.broadcasted_iota(i32, shape, 0).astype(f32).astype(bf16)
    one, zero = jnp.ones(shape, bf16), jnp.zeros(shape, bf16)
    labels = [jnp.clip(label_ref[...] - first, -1, 256).astype(f32).astype(bf16) for first in firsts]
    sums = [jnp.dot(jnp.where(ids == label, one, zero), rows_ref[...], preferred_element_type=f32) for label in labels]
    means = [(total * (1.0 / 64.0)).astype(bf16) for total in sums]
    coarse = [jnp.dot(mean, w_pool_ref[...], preferred_element_type=f32) for mean in means]
    inverse = [lax.rsqrt(jnp.mean(rows * rows, axis=1, keepdims=True) + 1e-06) for rows in coarse]
    return coarse, [(rows * scale * gain_ref[...]).astype(bf16) for rows, scale in zip(coarse, inverse)]


def query_kernel(first_ref, label_ref, rows_ref, w_pool_ref, gain_ref, w_query_ref, coarse_ref, query_ref):
    coarse, normed = normed_parents([first_ref[0]], label_ref, rows_ref, w_pool_ref, gain_ref, query_ref.shape[0])
    coarse_ref[...] = coarse[0]
    query_ref[...] = jnp.dot(normed[0], w_query_ref[...], preferred_element_type=f32).astype(bf16)


def key_kernel(label_ref, rows_ref, w_pool_ref, gain_ref, w_key_ref, w_value_ref, key_ref, value_ref):
    most = 256
    parts = value_ref.shape[0] // most
    firsts = [pl.program_id(0) * value_ref.shape[0] + part * most for part in range(parts)]
    normed = normed_parents(firsts, label_ref, rows_ref, w_pool_ref, gain_ref, most)[1]
    keys = [jnp.dot(rows, w_key_ref[...], preferred_element_type=f32) for rows in normed]
    values = [jnp.dot(rows, w_value_ref[...], preferred_element_type=f32) for rows in normed]
    for part in range(parts):
        at = slice(part * most, (part + 1) * most)
        value_ref[at, :] = values[part].astype(bf16)
        key_ref[:, at] = jnp.transpose(keys[part]).astype(bf16)


def halo_kernel(index_ref, own_ref, before_ref, after_ref):
    lane = lax.broadcasted_iota(i32, (128, 128), 1)
    wanted = [jnp.transpose(jnp.broadcast_to(index_ref[r:r + 1, :], (128, 128))) - lane for r in range(4)]
    step = 1024
    found = 0.0
    for start in range(0, own_ref.shape[0], step):
        hot = jnp.concatenate(
            [jnp.concatenate([(w == start + t).astype(f32).astype(bf16) for t in range(0, step, 128)], axis=1) for w in wanted],
            axis=0,
        )
        found += jnp.dot(hot, own_ref[start:start + step, :], preferred_element_type=f32)
    half = before_ref.shape[0]
    before_ref[...] = found[:half].astype(bf16)
    after_ref[...] = found[half:].astype(bf16)


def attend_kernel(factor_ref, key_ref, value_ref, *refs):
    query_refs, out_refs = refs[:len(refs) // 2], refs[len(refs) // 2:]
    rows = query_refs[0].shape[0]
    chunk = value_ref.shape[0] // 4
    chunks = [slice(c, c + chunk) for c in range(0, value_ref.shape[0], chunk)]
    ones = jnp.ones((chunk, 128), bf16)
    scores = []
    for g in range(2):
        scaled = jnp.concatenate(
            [ref[:, h * 128:(h + 1) * 128].astype(f32) * factor_ref[h] for ref in query_refs for h in range(4 * g, 4 * g + 4)],
            axis=0,
        )
        high = scaled.astype(bf16)
        low = (scaled - high.astype(f32)).astype(bf16)
        query = jnp.concatenate([high, low], axis=1)
        own = slice(g * 128, (g + 1) * 128)
        scores.append(
            [jnp.dot(query, jnp.concatenate([key_ref[own, c]] * 2, axis=0), preferred_element_type=f32) for c in chunks]
        )
    levels = [jnp.zeros((rows, 128), f32) for ref in out_refs]
    lanes = lax.broadcasted_iota(i32, (rows, 128), 1)
    for g in range(2):
        own = slice(g * 128, (g + 1) * 128)
        top = functools.reduce(jnp.maximum, [jnp.max(score, axis=1, keepdims=True) for score in scores[g]])
        both = 0.0
        for score, c in zip(scores[g], chunks):
            weight = jnp.exp2(score - top).astype(bf16)
            both += jnp.dot(weight, jnp.concatenate([value_ref[c, own], ones], axis=1), preferred_element_type=f32)
        norm = both[:, 128:]
        attn = (both[:, :128] / norm).astype(bf16)
        level = top + jnp.log2(norm)
        for n, out_ref in enumerate(out_refs):
            for r in range(4):
                h = 4 * g + r
                at = slice((4 * n + r) * rows, (4 * n + r + 1) * rows)
                out_ref[:, h * 128:(h + 1) * 128] = attn[at]
                levels[n] = jnp.where(lanes == h, level[at], levels[n])
    for level, out_ref in zip(levels, out_refs):
        high = level.astype(bf16)
        rest = level - high.astype(f32)
        middle = rest.astype(bf16)
        out_ref[:, 1024:1152] = high
        out_ref[:, 1152:1280] = middle
        out_ref[:, 1280:1408] = (rest - middle.astype(f32)).astype(bf16)


def merge_kernel(a_ref, b_ref, c_ref, d_ref, coarse_ref, w_out_ref, out_ref):
    refs = (a_ref, b_ref, c_ref, d_ref)
    levels = [r[:, 1024:1152].astype(f32) + (r[:, 1152:1280].astype(f32) + r[:, 1280:1408].astype(f32)) for r in refs]
    top = jnp.maximum(jnp.maximum(levels[0], levels[1]), jnp.maximum(levels[2], levels[3]))
    shares = [jnp.exp2(level - top) for level in levels]
    whole = shares[0] + shares[1] + shares[2] + shares[3]
    shares = [share / whole for share in shares]
    pieces = []
    for h in range(8):
        at = slice(h * 128, (h + 1) * 128)
        pieces.append(sum(r[:, at].astype(f32) * s[:, h:h + 1] for r, s in zip(refs, shares)))
    attn = jnp.concatenate(pieces, axis=1).astype(bf16)
    out_ref[...] = (coarse_ref[...] + jnp.dot(attn, w_out_ref[...], preferred_element_type=f32)).astype(bf16)


def body(fine_state, send_index, edge_src, edge_dst, cell_slot, slot_parent, w_src, w_dst, msg_bias, w_msg, w_upd,
         w_pool, norm_gain, w_query, w_key, w_value, w_out, head_scale):
    groups, devices = lax.axis_size("grp"), lax.axis_size("cur")
    smem = pl.BlockSpec(memory_space=pltpu.SMEM)
    vmem = pl.BlockSpec(memory_space=pltpu.VMEM)
    every = groups * devices
    both = ("grp", "cur")
    limit = lambda size: pltpu.CompilerParams(vmem_limit_bytes=size << 20)
    halo = send_index.shape[2]
    to_next, to_prev = pl.pallas_call(
        halo_kernel,
        out_shape=[jax.ShapeDtypeStruct((halo, fine_state.shape[1]), bf16)] * 2,
        in_specs=[vmem] * 2,
        out_specs=[vmem] * 2,
        compiler_params=limit(16),
        name="halo_cells",
    )(send_index.reshape(-1, 128), fine_state)
    before = lax.ppermute(to_next, both, [(i, (i + 1) % every) for i in range(every)])
    after = lax.ppermute(to_prev, both, [(i, (i - 1) % every) for i in range(every)])
    slots = slot_parent.shape[1]
    par_dev = slots - 1
    parents = jnp.pad(slot_parent, ((0, 0), (0, 256 - slots)), constant_values=-64)
    fine_out, part = fine_pass(fine_state, before, after, edge_src[0], edge_dst[0], cell_slot, parents,
                               w_src, w_dst, msg_bias, w_msg, w_upd)
    blocks = gather_group(part)
    labels = (blocks[:, slots, :SLOT_ROWS].astype(i32) * 64 + blocks[:, slots + 1, :SLOT_ROWS].astype(i32)).reshape(1, -1)
    rows = blocks.reshape(-1, 256)
    gain = norm_gain.reshape(1, -1)
    width = w_query.shape[1]
    coarse, query = pl.pallas_call(
        query_kernel,
        out_shape=(jax.ShapeDtypeStruct((par_dev, width), f32), jax.ShapeDtypeStruct((par_dev, width), bf16)),
        in_specs=[smem] + [vmem] * 5,
        out_specs=(vmem, vmem),
        compiler_params=limit(16),
        name="own_query",
    )((lax.axis_index("cur") * par_dev)[None], labels, rows, w_pool, gain, w_query)
    query, rows = lax.optimization_barrier((query, rows))
    asked = {by: lax.ppermute(query, "grp", [(i, (i + by) % groups) for i in range(groups)]) for by in (2, 1, 3)}
    asked[0] = query
    known = par_dev * devices
    step = 768
    whole = lambda *shape: pl.BlockSpec(shape, lambda i: (0,) * len(shape))
    keys, values = pl.pallas_call(
        key_kernel,
        out_shape=(jax.ShapeDtypeStruct((256, known), bf16), jax.ShapeDtypeStruct((known, 256), bf16)),
        grid=(known // step,),
        in_specs=[whole(*labels.shape), whole(*rows.shape), whole(*w_pool.shape), whole(*gain.shape),
                  whole(*w_key.shape), whole(*w_value.shape)],
        out_specs=(pl.BlockSpec((256, step), lambda i: (0, i)), pl.BlockSpec((step, 256), lambda i: (i, 0))),
        compiler_params=limit(32),
        name="group_keys",
    )(labels, rows, w_pool, gain, w_key, w_value)
    factor = head_scale * (math.log2(math.e) / math.sqrt(128.0))
    found = []
    for shifts in ((2,), (1, 3), (0,)):
        pieces = pl.pallas_call(
            attend_kernel,
            out_shape=[jax.ShapeDtypeStruct((par_dev, width + 384), bf16) for by in shifts],
            in_specs=[smem] + [vmem] * (2 + len(shifts)),
            out_specs=[vmem for by in shifts],
            compiler_params=limit(40),
            name="attend",
        )(factor, keys, values, *[asked[by] for by in shifts])
        for by, piece in zip(shifts, pieces):
            found.append(lax.ppermute(piece, "grp", [(i, (i - by) % groups) for i in range(groups)]) if by else piece)
    coarse_out = pl.pallas_call(
        merge_kernel,
        out_shape=jax.ShapeDtypeStruct((par_dev, width), bf16),
        in_specs=[vmem] * 6,
        out_specs=vmem,
        compiler_params=limit(12),
        name="merge",
    )(*found, coarse, w_out)
    return fine_out, coarse_out


def solution(mesh):
    line = P(("grp", "cur"), None)
    in_specs = (line, P(("grp", "cur"), None, None), line, line, P(("grp", "cur")), line) + (P(),) * 12
    return jax.shard_map(body, mesh=mesh, in_specs=in_specs, out_specs=(line, line), check_vma=False)
```

```python
import functools
import math
import jax, jax.numpy as jnp
from jax import lax
from jax.experimental import pallas as pl
from jax.experimental.pallas import tpu as pltpu
from jax.sharding import PartitionSpec as P

TILE = 256
WINDOW = 128
TOGETHER = 4
TARGET_SHIFT = 13
NO_TARGET = 6144
SLOT_ROWS = 104
SLOTS = 97
bf16, f32, i32 = jnp.bfloat16, jnp.float32, jnp.int32


def sort_kernel(source_ref, target_ref, rows_ref, targets_ref, key):
    given = source_ref.shape[0]
    fill = jnp.full((8, 128), NO_TARGET << TARGET_SHIFT, i32)
    held = [(target_ref[v] << TARGET_SHIFT) | source_ref[v] if v < given else fill for v in range(64)]
    for phase in range(1, 6):
        for bit in range(phase - 1, -1, -1):
            for v in range(64):
                if not v >> bit & 1:
                    w = v | 1 << bit
                    small, large = jnp.minimum(held[v], held[w]), jnp.maximum(held[v], held[w])
                    held[v], held[w] = (large, small) if v >> phase & 1 else (small, large)
    for v in range(64):
        key[v >> 3, v & 7] = held[v]
    row = lax.broadcasted_iota(i32, (8, 128), 0)
    lane = lax.broadcasted_iota(i32, (8, 128), 1)

    def bit_of(bit):
        if bit == 16:
            return jnp.zeros((8, 128), i32)
        return (row >> (bit - 6) & 1) if bit < 9 else (lane >> (bit - 9) & 1)

    for phase in range(6, 17):
        flip = bit_of(phase) if phase == 6 else bit_of(phase) ^ bit_of(phase - 1)

        def across(g, carry):
            held = key[pl.ds(2 * g, 2)].reshape(16, 8, 128) ^ (-flip)[None]
            for bit in range(phase - 1, 5, -1):
                axis, by, size = (1, 1 << (bit - 6), 8) if bit < 9 else (2, 1 << (bit - 9), 128)
                upper = (bit_of(bit) == 1)[None]
                if 2 * by == size:
                    other = pltpu.roll(held, by, axis)
                else:
                    other = jnp.where(upper, pltpu.roll(held, by, axis), pltpu.roll(held, size - by, axis))
                held = jnp.where(upper, jnp.maximum(held, other), jnp.minimum(held, other))
            key[pl.ds(2 * g, 2)] = held.reshape(2, 8, 8, 128)
            return carry

        lax.fori_loop(0, 4, across, 0, unroll=4)

        def merge(held):
            for bit in (2, 1, 0):
                pairs = held.reshape(4 >> bit, 2, 1 << bit, 8, 128)
                held = jnp.stack(
                    [jnp.minimum(pairs[:, 0], pairs[:, 1]), jnp.maximum(pairs[:, 0], pairs[:, 1])], axis=1
                ).reshape(8, 8, 128)
            return held

        def high(g, carry):
            key[:, g] = merge(key[:, g])
            return carry

        def low(g, carry):
            key[g] = merge(key[g])
            return carry

        lax.fori_loop(0, 8, high, 0, unroll=8)
        lax.fori_loop(0, 8, low, 0, unroll=8)

    flat = key.reshape(512, 128)
    half = rows_ref.shape[1] // 2
    for part in range(4):
        piece = jnp.concatenate([flat[pl.ds(s, 64, stride=8), :] for s in (2 * part, 2 * part + 1)], axis=0)
        piece = jnp.transpose(piece)[:half]
        at = (part % 2, pl.ds(part // 2, half, stride=2), slice(None))
        rows_ref[at] = (piece & ((1 << TARGET_SHIFT) - 1)) * 2
        targets_ref[at] = piece >> TARGET_SHIFT


def sorted_edges(source, target):
    edges = source.shape[0]
    shape = jax.ShapeDtypeStruct((2, edges // TILE, 128), i32)
    return pl.pallas_call(
        sort_kernel,
        out_shape=(shape, shape),
        scratch_shapes=[pltpu.VMEM((8, 8, 8, 128), i32)],
        compiler_params=pltpu.CompilerParams(vmem_limit_bytes=24 << 20),
        name="sort_edges",
    )(source.reshape(-1, 8, 128), target.reshape(-1, 8, 128))


def fine_kernel(rows_ref, start_ref, windows_ref, pairs_ref, local_ref, slot_ref, parent_ref, own_ref, before_ref, after_ref, w_src_ref, w_dst_ref,
                bias_ref, w_msg_ref, w_upd_ref, out_ref, part_ref, table, dst, total, count, got_a, got_b):
    blocks = own_ref.shape[0] // TILE
    tiles_most = local_ref.shape[1]

    def put_table(places, groups):
        projs = [jnp.dot(rows, w_src_ref[...], preferred_element_type=f32).astype(bf16).astype(f32) for rows in groups]
        for place, proj in zip(places, projs):
            proj = proj + bias_ref[...]
            table[pl.ds(2 * place, TILE, stride=2), :] = proj[:, :128]
            table[pl.ds(2 * place + 1, TILE, stride=2), :] = proj[:, 128:]

    def project(j, carry):
        places = [pl.multiple_of((j * TOGETHER + n) * TILE, TILE) for n in range(TOGETHER)]
        groups = [own_ref[pl.ds(at, TILE), :] for at in places]
        put_table(places, groups)
        mine = [jnp.dot(own, w_dst_ref[...], preferred_element_type=f32).astype(bf16) for own in groups]
        for at, proj in zip(places, mine):
            dst[pl.ds(at, TILE), :] = proj
            total[pl.ds(at, TILE), :] = jnp.zeros((TILE, 256), f32)
            count[pl.ds(at, TILE), :] = jnp.zeros((TILE, 128), f32)
        return carry

    lax.fori_loop(0, blocks // TOGETHER, project, 0)
    put_table((blocks * TILE, blocks * TILE + TILE), (before_ref[...], after_ref[...]))

    place = lax.broadcasted_iota(i32, (WINDOW, TILE), 0).astype(f32).astype(bf16)
    one, zero = jnp.ones((WINDOW, TILE), bf16), jnp.zeros((WINDOW, TILE), bf16)
    ones = jnp.ones((TILE, 128), bf16)

    def fetch(base, first, last, got):
        for i in range(first, last):
            place = i % TILE // 128 * (tiles_most * 128) + i // TILE * 128 + i % 128
            got[2 * i:2 * i + 2, :] = table[pl.ds(rows_ref[base + place], 2), :]

    def tile_steps(tile, n, got, start):
        state = {}

        def first():
            state["at"] = at = pl.multiple_of(start, 16)
            local = jnp.concatenate([local_ref[k, pl.ds(tile, 1), :] for k in range(2)], axis=1)
            local = jnp.minimum(local - at, WINDOW).astype(f32).astype(bf16)
            state["hot"] = jnp.where(place == local, one, zero)
            state["own"] = lax.dot_general(
                state["hot"], dst[pl.ds(at, WINDOW), :], (((0,), (0,)), ((), ())), preferred_element_type=f32
            )

        def second():
            sent = [got[pl.ds(2 * TILE * n + k, TILE, stride=2), :] for k in range(2)]
            half = 0.5 * (state["own"] + jnp.concatenate(sent, axis=1))
            state["hidden"] = (half + half * jnp.tanh(half)).astype(bf16)

        def third():
            at = pl.ds(state["at"], WINDOW)
            total[at, :] += jnp.dot(state["hot"], state["hidden"], preferred_element_type=f32)
            count[at, :] += jnp.dot(state["hot"], ones, preferred_element_type=f32)

        return first, second, third

    def advance(tile, got, ahead, got_ahead):
        base = jnp.minimum(ahead, tiles_most - TOGETHER) * 128
        tiles = [tile_steps(tile + n, n, got, start_ref[tile + n]) for n in range(TOGETHER)]
        steps = [run for steps in zip(*tiles) for run in steps]
        rows = TOGETHER * TILE
        for i, run in enumerate(steps):
            fetch(base, rows * i // len(steps), rows * (i + 1) // len(steps), got_ahead)
            run()

    def step(j, carry):
        tile = 2 * TOGETHER * j
        advance(tile, got_a, tile + TOGETHER, got_b)
        advance(tile + TOGETHER, got_b, tile + 2 * TOGETHER, got_a)
        return carry

    fetch(0, 0, TOGETHER * TILE, got_a)
    lax.fori_loop(0, pairs_ref[0], step, 0)

    def rest(tile, carry):
        def window(w, carry):
            fetch(tile * 128, 0, TILE, got_a)
            for run in tile_steps(tile, 0, got_a, jnp.minimum(start_ref[tile] + w * WINDOW, blocks * TILE - WINDOW)):
                run()
            return carry

        return lax.fori_loop(1, windows_ref[tile], window, carry)

    lax.fori_loop(0, tiles_most, rest, 0)

    slots = lax.broadcasted_iota(i32, (SLOT_ROWS, TILE), 0)

    row = lax.broadcasted_iota(i32, (SLOT_ROWS, 256), 0)
    high = jnp.where(row == SLOTS, parent_ref[...] >> 6, 0)
    tags = jnp.where(row == SLOTS + 1, parent_ref[...] & 63, high).astype(f32)

    def finish(j, parts):
        group = [j * TOGETHER + n for n in range(TOGETHER)]
        spots = [pl.ds(pl.multiple_of(b * TILE, TILE), TILE) for b in group]
        w_msg = w_msg_ref[...]
        highs, lows = [], []
        for at in spots:
            scale = 1.0 / jnp.maximum(count[at, :], 1.0)
            mean = total[at, :] * jnp.concatenate([scale, scale], axis=1)
            highs.append(mean.astype(bf16))
            lows.append((mean - highs[-1].astype(f32)).astype(bf16))
        aggs = [
            jnp.dot(high, w_msg, preferred_element_type=f32) + jnp.dot(low, w_msg, preferred_element_type=f32)
            for high, low in zip(highs, lows)
        ]
        updates = [jnp.dot(agg.astype(bf16), w_upd_ref[...], preferred_element_type=f32) for agg in aggs]
        for b, at, update in zip(group, spots, updates):
            new = (own_ref[at, :].astype(f32) + update).astype(bf16)
            out_ref[at, :] = new
            hot = (slots == slot_ref[b]).astype(f32).astype(bf16)
            parts += jnp.dot(hot, new, preferred_element_type=f32)
        return parts

    parts = lax.fori_loop(0, blocks // TOGETHER, finish, tags)
    part_ref[...] = parts.astype(bf16)


def fine_pass(own, before, after, source, target, cell_slot, parents, w_src, w_dst, bias, w_msg, w_upd):
    cells = own.shape[0]
    blocks = cells // TILE
    tiles = source.shape[0] // TILE
    rows, targets = sorted_edges(source, target)
    start = jnp.minimum(targets[0, :, 0] & -16, cells - WINDOW)
    last = jnp.max(jnp.where(targets < cells, targets, -1), axis=(0, 2))
    windows = jnp.maximum(last + WINDOW - start, 0) // WINDOW
    pairs = (jnp.sum((last >= 0).astype(i32)) + (2 * TOGETHER - 1)) // (2 * TOGETHER)
    smem = pl.BlockSpec(memory_space=pltpu.SMEM)
    vmem = pl.BlockSpec(memory_space=pltpu.VMEM)
    return pl.pallas_call(
        fine_kernel,
        out_shape=(jax.ShapeDtypeStruct(own.shape, bf16), jax.ShapeDtypeStruct((SLOT_ROWS, 256), bf16)),
        in_specs=[smem] * 4 + [vmem] * 11,
        out_specs=(vmem, vmem),
        scratch_shapes=[
            pltpu.VMEM((2 * (cells + 2 * TILE), 128), f32),
            pltpu.VMEM((cells, 256), bf16),
            pltpu.VMEM((cells, 256), f32),
            pltpu.VMEM((cells, 128), f32),
            pltpu.VMEM((2 * TOGETHER * TILE, 128), f32),
            pltpu.VMEM((2 * TOGETHER * TILE, 128), f32),
        ],
        compiler_params=pltpu.CompilerParams(vmem_limit_bytes=58 << 20),
        name="fine_cells",
    )(rows.reshape(-1), start, windows, pairs[None], targets, cell_slot.reshape(blocks, 1, TILE), parents, own, before, after, w_src, w_dst,
      bias.reshape(1, -1), w_msg, w_upd)


def moved(value, axis, pairs):
    return lax.ppermute(value, axis, pairs)


def ring_gather(value, move):
    return jnp.concatenate([value] + [move(value, by) for by in (1, 3, 2)], axis=0)


def gather_group(part):
    devices = lax.axis_size("cur")

    def along_z(value, by):
        return lax.ppermute(value, "cur", [(i, i // 8 * 8 + (i + 2 * by) % 8) for i in range(devices)])

    def along_x(value, by):
        return lax.ppermute(value, "cur", [(i, (i + 8 * by) % devices) for i in range(devices)])

    rows = ring_gather(part[None], along_z)
    rows = ring_gather(rows, along_x)
    return jnp.concatenate([rows, lax.ppermute(rows, "cur", [(i, i ^ 1) for i in range(devices)])], axis=0)


def normed_parents(firsts, label_ref, rows_ref, w_pool_ref, gain_ref, parents):
    shape = (parents, rows_ref.shape[0])
    ids = lax.broadcasted_iota(i32, shape, 0).astype(f32).astype(bf16)
    one, zero = jnp.ones(shape, bf16), jnp.zeros(shape, bf16)
    labels = [jnp.clip(label_ref[...] - first, -1, 256).astype(f32).astype(bf16) for first in firsts]
    sums = [jnp.dot(jnp.where(ids == label, one, zero), rows_ref[...], preferred_element_type=f32) for label in labels]
    means = [(total * (1.0 / 64.0)).astype(bf16) for total in sums]
    coarse = [jnp.dot(mean, w_pool_ref[...], preferred_element_type=f32) for mean in means]
    inverse = [lax.rsqrt(jnp.mean(rows * rows, axis=1, keepdims=True) + 1e-06) for rows in coarse]
    return coarse, [(rows * scale * gain_ref[...]).astype(bf16) for rows, scale in zip(coarse, inverse)]


def query_kernel(first_ref, label_ref, rows_ref, w_pool_ref, gain_ref, w_query_ref, coarse_ref, query_ref):
    coarse, normed = normed_parents([first_ref[0]], label_ref, rows_ref, w_pool_ref, gain_ref, query_ref.shape[0])
    coarse_ref[...] = coarse[0]
    query_ref[...] = jnp.dot(normed[0], w_query_ref[...], preferred_element_type=f32).astype(bf16)


def key_kernel(label_ref, rows_ref, w_pool_ref, gain_ref, w_key_ref, w_value_ref, key_ref, value_ref):
    most = 256
    parts = value_ref.shape[0] // most
    firsts = [pl.program_id(0) * value_ref.shape[0] + part * most for part in range(parts)]
    normed = normed_parents(firsts, label_ref, rows_ref, w_pool_ref, gain_ref, most)[1]
    keys = [jnp.dot(rows, w_key_ref[...], preferred_element_type=f32) for rows in normed]
    values = [jnp.dot(rows, w_value_ref[...], preferred_element_type=f32) for rows in normed]
    for part in range(parts):
        at = slice(part * most, (part + 1) * most)
        value_ref[at, :] = values[part].astype(bf16)
        key_ref[:, at] = jnp.transpose(keys[part]).astype(bf16)


def halo_kernel(index_ref, own_ref, before_ref, after_ref):
    lane = lax.broadcasted_iota(i32, (128, 128), 1)
    wanted = [jnp.transpose(jnp.broadcast_to(index_ref[r:r + 1, :], (128, 128))) - lane for r in range(4)]
    step = 1024
    found = 0.0
    for start in range(0, own_ref.shape[0], step):
        hot = jnp.concatenate(
            [jnp.concatenate([(w == start + t).astype(f32).astype(bf16) for t in range(0, step, 128)], axis=1) for w in wanted],
            axis=0,
        )
        found += jnp.dot(hot, own_ref[start:start + step, :], preferred_element_type=f32)
    half = before_ref.shape[0]
    before_ref[...] = found[:half].astype(bf16)
    after_ref[...] = found[half:].astype(bf16)


def attend_kernel(factor_ref, key_ref, value_ref, *refs):
    query_refs, out_refs = refs[:len(refs) // 2], refs[len(refs) // 2:]
    rows = query_refs[0].shape[0]
    chunk = value_ref.shape[0] // 4
    chunks = [slice(c, c + chunk) for c in range(0, value_ref.shape[0], chunk)]
    ones = jnp.ones((chunk, 128), bf16)
    scores = []
    for g in range(2):
        scaled = jnp.concatenate(
            [ref[:, h * 128:(h + 1) * 128].astype(f32) * factor_ref[h] for ref in query_refs for h in range(4 * g, 4 * g + 4)],
            axis=0,
        )
        high = scaled.astype(bf16)
        low = (scaled - high.astype(f32)).astype(bf16)
        query = jnp.concatenate([high, low], axis=1)
        own = slice(g * 128, (g + 1) * 128)
        scores.append(
            [jnp.dot(query, jnp.concatenate([key_ref[own, c]] * 2, axis=0), preferred_element_type=f32) for c in chunks]
        )
    levels = [jnp.zeros((rows, 128), f32) for ref in out_refs]
    lanes = lax.broadcasted_iota(i32, (rows, 128), 1)
    for g in range(2):
        own = slice(g * 128, (g + 1) * 128)
        top = functools.reduce(jnp.maximum, [jnp.max(score, axis=1, keepdims=True) for score in scores[g]])
        both = 0.0
        for score, c in zip(scores[g], chunks):
            weight = jnp.exp2(score - top).astype(bf16)
            both += jnp.dot(weight, jnp.concatenate([value_ref[c, own], ones], axis=1), preferred_element_type=f32)
        norm = both[:, 128:]
        attn = (both[:, :128] / norm).astype(bf16)
        level = top + jnp.log2(norm)
        for n, out_ref in enumerate(out_refs):
            for r in range(4):
                h = 4 * g + r
                at = slice((4 * n + r) * rows, (4 * n + r + 1) * rows)
                out_ref[:, h * 128:(h + 1) * 128] = attn[at]
                levels[n] = jnp.where(lanes == h, level[at], levels[n])
    for level, out_ref in zip(levels, out_refs):
        high = level.astype(bf16)
        rest = level - high.astype(f32)
        middle = rest.astype(bf16)
        out_ref[:, 1024:1152] = high
        out_ref[:, 1152:1280] = middle
        out_ref[:, 1280:1408] = (rest - middle.astype(f32)).astype(bf16)


def merge_kernel(a_ref, b_ref, c_ref, d_ref, coarse_ref, w_out_ref, out_ref):
    refs = (a_ref, b_ref, c_ref, d_ref)
    levels = [r[:, 1024:1152].astype(f32) + (r[:, 1152:1280].astype(f32) + r[:, 1280:1408].astype(f32)) for r in refs]
    top = jnp.maximum(jnp.maximum(levels[0], levels[1]), jnp.maximum(levels[2], levels[3]))
    shares = [jnp.exp2(level - top) for level in levels]
    whole = shares[0] + shares[1] + shares[2] + shares[3]
    shares = [share / whole for share in shares]
    pieces = []
    for h in range(8):
        at = slice(h * 128, (h + 1) * 128)
        pieces.append(sum(r[:, at].astype(f32) * s[:, h:h + 1] for r, s in zip(refs, shares)))
    attn = jnp.concatenate(pieces, axis=1).astype(bf16)
    out_ref[...] = (coarse_ref[...] + jnp.dot(attn, w_out_ref[...], preferred_element_type=f32)).astype(bf16)


def body(fine_state, send_index, edge_src, edge_dst, cell_slot, slot_parent, w_src, w_dst, msg_bias, w_msg, w_upd,
         w_pool, norm_gain, w_query, w_key, w_value, w_out, head_scale):
    groups, devices = lax.axis_size("grp"), lax.axis_size("cur")
    smem = pl.BlockSpec(memory_space=pltpu.SMEM)
    vmem = pl.BlockSpec(memory_space=pltpu.VMEM)
    every = groups * devices
    both = ("grp", "cur")
    limit = lambda size: pltpu.CompilerParams(vmem_limit_bytes=size << 20)
    halo = send_index.shape[2]
    to_next, to_prev = pl.pallas_call(
        halo_kernel,
        out_shape=[jax.ShapeDtypeStruct((halo, fine_state.shape[1]), bf16)] * 2,
        in_specs=[vmem] * 2,
        out_specs=[vmem] * 2,
        compiler_params=limit(16),
        name="halo_cells",
    )(send_index.reshape(-1, 128), fine_state)
    before = lax.ppermute(to_next, both, [(i, (i + 1) % every) for i in range(every)])
    after = lax.ppermute(to_prev, both, [(i, (i - 1) % every) for i in range(every)])
    slots = slot_parent.shape[1]
    par_dev = slots - 1
    parents = jnp.pad(slot_parent, ((0, 0), (0, 256 - slots)), constant_values=-64)
    fine_out, part = fine_pass(fine_state, before, after, edge_src[0], edge_dst[0], cell_slot, parents,
                               w_src, w_dst, msg_bias, w_msg, w_upd)
    blocks = gather_group(part)
    labels = (blocks[:, slots, :SLOT_ROWS].astype(i32) * 64 + blocks[:, slots + 1, :SLOT_ROWS].astype(i32)).reshape(1, -1)
    rows = blocks.reshape(-1, 256)
    gain = norm_gain.reshape(1, -1)
    width = w_query.shape[1]
    coarse, query = pl.pallas_call(
        query_kernel,
        out_shape=(jax.ShapeDtypeStruct((par_dev, width), f32), jax.ShapeDtypeStruct((par_dev, width), bf16)),
        in_specs=[smem] + [vmem] * 5,
        out_specs=(vmem, vmem),
        compiler_params=limit(16),
        name="own_query",
    )((lax.axis_index("cur") * par_dev)[None], labels, rows, w_pool, gain, w_query)
    query, rows = lax.optimization_barrier((query, rows))
    asked = {by: lax.ppermute(query, "grp", [(i, (i + by) % groups) for i in range(groups)]) for by in (1, 3, 2)}
    asked[0] = query
    known = par_dev * devices
    step = 768
    whole = lambda *shape: pl.BlockSpec(shape, lambda i: (0,) * len(shape))
    keys, values = pl.pallas_call(
        key_kernel,
        out_shape=(jax.ShapeDtypeStruct((256, known), bf16), jax.ShapeDtypeStruct((known, 256), bf16)),
        grid=(known // step,),
        in_specs=[whole(*labels.shape), whole(*rows.shape), whole(*w_pool.shape), whole(*gain.shape),
                  whole(*w_key.shape), whole(*w_value.shape)],
        out_specs=(pl.BlockSpec((256, step), lambda i: (0, i)), pl.BlockSpec((step, 256), lambda i: (i, 0))),
        compiler_params=limit(32),
        name="group_keys",
    )(labels, rows, w_pool, gain, w_key, w_value)
    factor = head_scale * (math.log2(math.e) / math.sqrt(128.0))
    found = []
    for shifts in ((1, 3), (2,), (0,)):
        pieces = pl.pallas_call(
            attend_kernel,
            out_shape=[jax.ShapeDtypeStruct((par_dev, width + 384), bf16) for by in shifts],
            in_specs=[smem] + [vmem] * (2 + len(shifts)),
            out_specs=[vmem for by in shifts],
            compiler_params=limit(40),
            name="attend",
        )(factor, keys, values, *[asked[by] for by in shifts])
        for by, piece in zip(shifts, pieces):
            found.append(lax.ppermute(piece, "grp", [(i, (i - by) % groups) for i in range(groups)]) if by else piece)
    coarse_out = pl.pallas_call(
        merge_kernel,
        out_shape=jax.ShapeDtypeStruct((par_dev, width), bf16),
        in_specs=[vmem] * 6,
        out_specs=vmem,
        compiler_params=limit(12),
        name="merge",
    )(*found, coarse, w_out)
    return fine_out, coarse_out


def solution(mesh):
    line = P(("grp", "cur"), None)
    in_specs = (line, P(("grp", "cur"), None, None), line, line, P(("grp", "cur")), line) + (P(),) * 12
    return jax.shard_map(body, mesh=mesh, in_specs=in_specs, out_specs=(line, line), check_vma=False)
```
